32 devices in a mesh: ctx: 8 (over y, x, core), head: 4 (over z).
Axes of the slice: x: 2, y: 2, z: 4, core: 2. Of those that a mesh axis runs over, the one named last changes fastest.
Arguments:
- queries: bfloat16 [8192, 1024], P('ctx', 'head'), may hold values from -8 to 8
- keys: bfloat16 [8192, 256], P('ctx'), may hold values from -8 to 8
- values: bfloat16 [8192, 256], P('ctx'), may hold values from -8 to 8
- grad_out: bfloat16 [8192, 1024], P('ctx', 'head'), may hold values from -8 to 8
- block_index: int32 [8, 3], replicated, may hold values from 0 to 3
Outputs:
- grad_queries: bfloat16 [8192, 1024], P(('ctx', 'head'))
- grad_keys: bfloat16 [8192, 256], P(('ctx', 'head'))
- grad_values: bfloat16 [8192, 256], P(('ctx', 'head'))
The draws below stay inside these ranges and needn't reach their ends.
Inputs may be any that keep to these rules, and one draw needn't show every extreme that they name: block_index[c, l] is read only where c >= 2**l.
All inputs are finite; a program needn't handle non-finite values.
Results may differ from the reference program's by a relative error of at most 0.023.
Values may be sent and summed in bfloat16 or wider, within the bound.
A program may use at most 64 MiB of HBM per device.

```python
import jax
import jax.numpy as jnp
from jax import lax

HD = 128
GROUP = 4
BLK = 256
SHARD = 1024
HQ = 8
KVH = 2
TOKENS = 8192
LEVELS = 3
N_CTX = 8


def shared_keys(key):
    drawn = jnp.clip(jax.random.normal(jax.random.fold_in(key, 11), (TOKENS, KVH * HD), jnp.float32), -8.0, 8.0)
    return drawn


def draw_keys(key, part):
    return shared_keys(key).astype(jnp.bfloat16)


def draw_queries(key, part):
    drawn = jnp.clip(jax.random.normal(jax.random.fold_in(key, 21), (TOKENS, HQ * HD), jnp.float32), -8.0, 8.0)
    return drawn.astype(jnp.bfloat16)


def set_ends(values, own_key, low, top_value):
    longest = values.shape.index(max(values.shape))
    spots = []
    for shift in (0, 1):
        where = [jax.random.randint(jax.random.fold_in(own_key, axis), (), 0, length) for axis, length in enumerate(values.shape)]
        where[longest] = (where[longest] + shift) % values.shape[longest]
        spots.append(tuple(where))
    return values.at[spots[0]].set(low).at[spots[1]].set(top_value)


def steps_of(own_key, shape, split, least, high):
    def one(position, shards_of):
        heights = jax.random.uniform(jax.random.fold_in(jax.random.fold_in(own_key, 6), position), (shards_of,), jnp.float32, least / len(split), high / len(split))
        return jnp.repeat(jnp.exp(heights), shape[position] // shards_of).reshape((-1,) + (1,) * (len(shape) - position - 1))

    level = one(*split[0])
    for cut in split[1:]:
        level = level * one(*cut)
    return level


def centred(rng, dims, scale, limit, split=(), dtype=jnp.bfloat16):
    gain = steps_of(rng, dims, split, -0.22, 0.18) if split else 1.0
    values = jax.random.normal(rng, dims, jnp.float32) * scale * gain
    return jnp.minimum(jnp.maximum(values, -limit), limit).astype(dtype)


def setup_inputs(seed: int = 0) -> dict:
    seeds = jax.random.split(jax.random.key(seed), 6)
    return {
        "queries": draw_queries(jax.random.fold_in(seeds[5], 71), 0),
        "keys": draw_keys(jax.random.fold_in(seeds[5], 71), 0),
        "values": centred(seeds[2], (TOKENS, KVH * HD), 1.0, 8.0, ((0, 8),)),
        "grad_out": centred(seeds[3], (TOKENS, HQ * HD), 1.0, 8.0, ((0, 8), (1, 4))),
        "block_index": set_ends(jax.random.randint(seeds[4], (N_CTX, LEVELS), 0, SHARD // BLK), jax.random.fold_in(seeds[4], 1), 0, (SHARD // BLK) - 1).astype(jnp.int32),
    }


def head_grads(query_group, key_group, value_group, grad_group, visible):
    softmax_scale = HD ** -0.5
    query_full = query_group.astype(jnp.float32)
    key_full = key_group.astype(jnp.float32)
    value_full = value_group.astype(jnp.float32)
    grad_full = grad_group.astype(jnp.float32)
    scores = jnp.einsum('hqd,kd->hqk', query_full, key_full) * softmax_scale
    scores = jnp.where(visible[None], scores, -jnp.inf)
    row_max = jnp.max(scores, axis=-1, keepdims=True)
    weights = jnp.exp(scores - row_max)
    probs = weights / jnp.sum(weights, axis=-1, keepdims=True)
    probs_low = probs.astype(jnp.bfloat16)
    grad_probs = jnp.einsum('hqd,kd->hqk', grad_full, value_full)
    delta = jnp.sum(probs * grad_probs, axis=-1, keepdims=True)
    scores_low = (probs * (grad_probs - delta)).astype(jnp.bfloat16)
    scores_full = scores_low.astype(jnp.float32)
    grad_query = (softmax_scale * jnp.einsum('hqk,kd->hqd', scores_full, key_full)).astype(jnp.bfloat16)
    grad_key = softmax_scale * jnp.einsum('hqk,hqd->kd', scores_full, query_full)
    grad_value = jnp.einsum('hqk,hqd->kd', probs_low.astype(jnp.float32), grad_full)
    return grad_query, grad_key, grad_value


def reference(queries, keys, values, grad_out, block_index):
    levels = N_CTX.bit_length() - 1
    query_split = queries.reshape(N_CTX, SHARD, KVH, GROUP, HD)
    grad_split = grad_out.reshape(N_CTX, SHARD, KVH, GROUP, HD)
    key_split = keys.reshape(N_CTX, SHARD, KVH, HD)
    value_split = values.reshape(N_CTX, SHARD, KVH, HD)
    key_total = jnp.zeros((N_CTX, SHARD, KVH, HD), jnp.float32)
    value_total = jnp.zeros((N_CTX, SHARD, KVH, HD), jnp.float32)
    causal = jnp.arange(SHARD)[None, :] <= jnp.arange(SHARD)[:, None]
    dq_parts = []
    for shard_idx in range(N_CTX):
        key_parts = [key_split[shard_idx]]
        value_parts = [value_split[shard_idx]]
        mask_parts = [causal]
        begins = []
        for level_num in range(levels):
            distance = 2 ** level_num
            source = max(shard_idx - distance, 0)
            block_begin = (block_index[shard_idx, level_num] * BLK).astype(jnp.int32)
            key_parts.append(lax.dynamic_slice_in_dim(key_split[source], block_begin, BLK, 0))
            value_parts.append(lax.dynamic_slice_in_dim(value_split[source], block_begin, BLK, 0))
            mask_parts.append(jnp.full((SHARD, BLK), shard_idx >= distance))
            begins.append(block_begin)
        key_all = jnp.concatenate(key_parts, axis=0)
        value_all = jnp.concatenate(value_parts, axis=0)
        visible = jnp.concatenate(mask_parts, axis=1)
        query_heads = jnp.transpose(query_split[shard_idx], (1, 2, 0, 3))
        grad_heads = jnp.transpose(grad_split[shard_idx], (1, 2, 0, 3))
        key_heads = jnp.transpose(key_all, (1, 0, 2))
        value_heads = jnp.transpose(value_all, (1, 0, 2))
        grad_query, grad_key, grad_value = lax.map(
            lambda items: head_grads(items[0], items[1], items[2], items[3], visible),
            (query_heads, key_heads, value_heads, grad_heads))
        dq_parts.append(jnp.transpose(grad_query, (2, 0, 1, 3)).reshape(SHARD, HQ * HD))
        key_rows = jnp.transpose(grad_key, (1, 0, 2))
        value_rows = jnp.transpose(grad_value, (1, 0, 2))
        key_total = key_total.at[shard_idx].add(key_rows[:SHARD])
        value_total = value_total.at[shard_idx].add(value_rows[:SHARD])
        for level_num in range(levels):
            source = max(shard_idx - 2 ** level_num, 0)
            lower = SHARD + level_num * BLK
            block_begin = begins[level_num]
            current = lax.dynamic_slice_in_dim(key_total[source], block_begin, BLK, 0)
            key_total = key_total.at[source].set(lax.dynamic_update_slice_in_dim(key_total[source], current + key_rows[lower:lower + BLK], block_begin, 0))
            current = lax.dynamic_slice_in_dim(value_total[source], block_begin, BLK, 0)
            value_total = value_total.at[source].set(lax.dynamic_update_slice_in_dim(value_total[source], current + value_rows[lower:lower + BLK], block_begin, 0))
    grad_queries = jnp.concatenate(dq_parts, axis=0)
    grad_keys = key_total.reshape(TOKENS, KVH * HD).astype(jnp.bfloat16)
    grad_values = value_total.reshape(TOKENS, KVH * HD).astype(jnp.bfloat16)
    return (grad_queries, grad_keys, grad_values)
```

```python
import functools

import jax
import jax.numpy as jnp
from jax import lax
from jax.experimental import pallas as pl
from jax.experimental.pallas import tpu as pltpu
from jax.sharding import PartitionSpec as P

HD = 128
BLK = 256
LOG2E = 1.4426950408889634
MESH = pl.DeviceIdType.MESH
NT = (((1,), (1,)), ((), ()))
NN = (((1,), (0,)), ((), ()))


def dot(a, b, dims=NN):
    return lax.dot_general(a, b, dims, preferred_element_type=jnp.float32)


def kernel(
    sizes,
    q_ref,
    do_ref,
    k_ref,
    v_ref,
    index_ref,
    dq_out,
    gk_out,
    gv_out,
    own_kv,
    own_kt,
    part_kt,
    kv_send,
    kv_recv,
    w_own,
    dp_own,
    w_part,
    dp_part,
    dq_part,
    acc,
    acc_part,
    ret_send,
    ret_recv,
    dq_stage,
    pair_send,
    pair_recv,
    final,
    kv_ssem,
    kv_rsem,
    ret_ssem,
    ret_rsem,
    dq_ssem,
    dq_rsem,
    pair_ssem,
    pair_rsem,
    fin_ssem,
    fin_rsem,
):
    n_ctx, n_head, kv_heads, local_heads, shard_rows, levels = sizes
    repl = n_head // kv_heads
    per_member = n_head // repl
    rows_out = shard_rows // n_head
    tiles = shard_rows // BLK
    cols = local_heads * BLK
    width = local_heads * HD
    scale = HD ** (-0.5)
    c2 = scale * LOG2E
    ctx = lax.axis_index("ctx")
    head = lax.axis_index("head")
    group = head // repl
    member = head % repl
    gcol = pl.multiple_of(group * HD, HD)

    barrier = pltpu.get_barrier_semaphore()
    greet = n_head - 1
    for level in range(levels):
        step = 2**level

        @pl.when(ctx + step < n_ctx)
        def _():
            pl.semaphore_signal(barrier, inc=1, device_id=(ctx + step, head), device_id_type=MESH)

        @pl.when(ctx >= step)
        def _():
            pl.semaphore_signal(barrier, inc=1, device_id=(ctx - step, head), device_id_type=MESH)

        greet = greet + jnp.where(ctx + step < n_ctx, 1, 0) + jnp.where(ctx >= step, 1, 0)
    for off in range(1, n_head):
        pl.semaphore_signal(
            barrier, inc=1, device_id=(ctx, (head + off) % n_head), device_id_type=MESH
        )

    own_kv[:, :HD] = k_ref[:, pl.ds(gcol, HD)]
    own_kv[:, HD:] = v_ref[:, pl.ds(gcol, HD)]
    blocks = []

    def is_block(level, block):
        return (blocks[level] == block).astype(jnp.float32)

    for level in range(levels):
        target = jnp.minimum(ctx + 2**level, n_ctx - 1)
        blocks.append(index_ref[target, level])
        chosen = jnp.zeros((BLK, 2 * HD), jnp.float32)
        for block in range(tiles):
            piece = own_kv[block * BLK : (block + 1) * BLK, :].astype(jnp.float32)
            chosen = chosen + piece * is_block(level, block)
        kv_send[level] = chosen.astype(jnp.bfloat16)

    pl.semaphore_wait(barrier, greet)

    def kv_copy(level):
        return pltpu.make_async_remote_copy(
            src_ref=kv_send.at[level],
            dst_ref=kv_recv.at[level],
            send_sem=kv_ssem.at[level],
            recv_sem=kv_rsem.at[level],
            device_id=(jnp.minimum(ctx + 2**level, n_ctx - 1), head),
            device_id_type=MESH,
        )

    for level in reversed(range(levels)):

        @pl.when(ctx + 2**level < n_ctx)
        def _():
            kv_copy(level).start()

        @pl.when(ctx < 2**level)
        def _():
            kv_recv[level] = jnp.zeros((BLK, 2 * HD), jnp.bfloat16)

        @pl.when(ctx + 2**level >= n_ctx)
        def _():
            ret_recv[level] = jnp.zeros((BLK, 2 * HD), jnp.bfloat16)

    def stacked(ref, tile):
        rows = pl.ds(tile * BLK, BLK)
        return jnp.concatenate(
            [ref[rows, h * HD : (h + 1) * HD] for h in range(local_heads)], axis=0
        )

    def slot(tile, block):
        return tile * (tile + 1) // 2 + block

    order = list(reversed(range(tiles)))
    key_pos = lax.broadcasted_iota(jnp.int32, (BLK, cols), 0)
    query_pos = lax.broadcasted_iota(jnp.int32, (BLK, cols), 1) % BLK
    for block in range(tiles):
        rows = pl.ds(block * BLK, BLK)
        own_kt[:, rows] = own_kv[rows, :HD].T

    own_stats = {}
    for tile in order:
        q_cat, do_cat = stacked(q_ref, tile), stacked(do_ref, tile)
        top = None
        for block in range(tile + 1):
            s = dot(own_kv[block * BLK : (block + 1) * BLK, :HD], q_cat, NT)
            if block == tile:
                s = jnp.where(key_pos <= query_pos, s, -1e30)
            w_own[slot(tile, block)] = s
            high = jnp.max(s, axis=0, keepdims=True)
            top = high if top is None else jnp.maximum(top, high)
        top = top * c2
        total = jnp.zeros((1, cols), jnp.float32)
        mixed = jnp.zeros((1, cols), jnp.float32)
        for block in range(tile + 1):
            w = jnp.exp2(w_own[slot(tile, block)] * c2 - top)
            dp = dot(own_kv[block * BLK : (block + 1) * BLK, HD:], do_cat, NT)
            w_own[slot(tile, block)] = w
            dp_own[slot(tile, block)] = dp
            total = total + jnp.sum(w, axis=0, keepdims=True)
            mixed = mixed + jnp.sum(w * dp, axis=0, keepdims=True)
        own_stats[tile] = (top, total, mixed)

    for level in range(levels):

        @pl.when(ctx >= 2**level)
        def _():
            kv_copy(level).wait_recv()

    dead = []
    for level in range(levels):
        part_kt[:, level * BLK : (level + 1) * BLK] = kv_recv[level, :, :HD].T
        dead.append(jnp.where(ctx >= 2**level, 0.0, 1e30).astype(jnp.float32))

    final_stats = {}
    for tile in order:
        q_cat, do_cat = stacked(q_ref, tile), stacked(do_ref, tile)
        top_own, total_own, mixed_own = own_stats[tile]
        top = top_own
        for level in range(levels):
            s = dot(kv_recv[level, :, :HD], q_cat, NT)
            w_part[level] = s
            top = jnp.maximum(top, jnp.max(s, axis=0, keepdims=True) * c2 - dead[level])
        keep = jnp.exp2(top_own - top)
        total = total_own * keep
        mixed = mixed_own * keep
        for level in range(levels):
            w = jnp.exp2(w_part[level] * c2 - (top + dead[level]))
            dp = dot(kv_recv[level, :, HD:], do_cat, NT)
            w_part[level] = w
            dp_part[level] = dp
            total = total + jnp.sum(w, axis=0, keepdims=True)
            mixed = mixed + jnp.sum(w * dp, axis=0, keepdims=True)
        inverse = 1.0 / total
        delta = mixed * inverse
        final_stats[tile] = (keep * inverse, delta)
        dq_t = None
        for level in range(levels):
            p = w_part[level] * inverse
            ds = (p * (dp_part[level] - delta)).astype(jnp.bfloat16)
            d_value = dot(p.astype(jnp.bfloat16), do_cat)
            d_key = dot(ds, q_cat) * scale
            if tile == order[0]:
                acc_part[level, :, :HD] = d_key
                acc_part[level, :, HD:] = d_value
            else:
                acc_part[level, :, :HD] += d_key
                acc_part[level, :, HD:] += d_value
            piece = dot(part_kt[:, level * BLK : (level + 1) * BLK], ds)
            dq_t = piece if dq_t is None else dq_t + piece
        dq_part[tile] = dq_t

    def ret_copy(level):
        return pltpu.make_async_remote_copy(
            src_ref=ret_send.at[level],
            dst_ref=ret_recv.at[level],
            send_sem=ret_ssem.at[level],
            recv_sem=ret_rsem.at[level],
            device_id=(jnp.maximum(ctx - 2**level, 0), head),
            device_id_type=MESH,
        )

    for level in reversed(range(levels)):
        ret_send[level] = acc_part[level].astype(jnp.bfloat16)

        @pl.when(ctx >= 2**level)
        def _():
            ret_copy(level).start()

    def dq_copy(dest, source):
        return pltpu.make_async_remote_copy(
            src_ref=dq_stage.at[pl.ds(dest * rows_out, rows_out), :],
            dst_ref=dq_out.at[:, pl.ds(pl.multiple_of(source * width, width), width)],
            send_sem=dq_ssem.at[dest],
            recv_sem=dq_rsem.at[source],
            device_id=(ctx, dest),
            device_id_type=MESH,
        )

    for tile in order:
        q_cat, do_cat = stacked(q_ref, tile), stacked(do_ref, tile)
        inverse, delta = final_stats[tile]
        dq_t = dq_part[tile]
        for block in range(tile + 1):
            p = w_own[slot(tile, block)] * inverse
            ds = (p * (dp_own[slot(tile, block)] - delta)).astype(jnp.bfloat16)
            d_value = dot(p.astype(jnp.bfloat16), do_cat)
            d_key = dot(ds, q_cat) * scale
            rows = slice(block * BLK, (block + 1) * BLK)
            if tile == order[0]:
                acc[rows, :HD] = d_key
                acc[rows, HD:] = d_value
            else:
                acc[rows, :HD] += d_key
                acc[rows, HD:] += d_value
            dq_t = dq_t + dot(own_kt[:, rows], ds)
        dq_t = dq_t * scale
        for h in range(local_heads):
            dq_stage[tile * BLK : (tile + 1) * BLK, h * HD : (h + 1) * HD] = (
                dq_t[:, h * BLK : (h + 1) * BLK].T.astype(jnp.bfloat16)
            )
        for dest in range(tile * BLK // rows_out, (tile + 1) * BLK // rows_out):

            @pl.when(head != dest)
            def _():
                dq_copy(dest, head).start()

            @pl.when(head == dest)
            def _():
                dq_out[:, pl.ds(pl.multiple_of(head * width, width), width)] = dq_stage[
                    dest * rows_out : (dest + 1) * rows_out, :
                ]

    for level in range(levels):

        @pl.when(ctx + 2**level < n_ctx)
        def _():
            ret_copy(level).wait_recv()

    for block in range(tiles):
        rows = slice(block * BLK, (block + 1) * BLK)
        value = acc[rows, :]
        for level in range(levels):
            back = ret_recv[level].astype(jnp.float32)
            value = value + back * is_block(level, block)
        acc[rows, :] = value

    def pair_copy(off, k):
        return pltpu.make_async_remote_copy(
            src_ref=pair_send.at[off - 1, k],
            dst_ref=pair_recv.at[off - 1, k],
            send_sem=pair_ssem.at[off - 1, k],
            recv_sem=pair_rsem.at[off - 1, k],
            device_id=(ctx, group * repl + (member + off) % repl),
            device_id_type=MESH,
        )

    for k in range(per_member):
        for off in range(1, repl):
            begin = pl.multiple_of((k * repl + (member + off) % repl) * rows_out, rows_out)
            pair_send[off - 1, k] = acc[pl.ds(begin, rows_out), :].astype(jnp.bfloat16)
            pair_copy(off, k).start()

    def fin_copy(part, k, source_group):
        out = (gk_out, gv_out)[part]
        return pltpu.make_async_remote_copy(
            src_ref=final.at[part, k],
            dst_ref=out.at[:, pl.ds(pl.multiple_of(source_group * HD, HD), HD)],
            send_sem=fin_ssem.at[part, k],
            recv_sem=fin_rsem.at[part, source_group],
            device_id=(ctx, k * repl + member),
            device_id_type=MESH,
        )

    for k in range(per_member):
        begin = pl.multiple_of((k * repl + member) * rows_out, rows_out)
        value = acc[pl.ds(begin, rows_out), :]
        for off in range(1, repl):
            pair_copy(off, k).wait_recv()
            value = value + pair_recv[off - 1, k].astype(jnp.float32)
        final[0, k] = value[:, :HD].astype(jnp.bfloat16)
        final[1, k] = value[:, HD:].astype(jnp.bfloat16)

        @pl.when(group != k)
        def _():
            fin_copy(0, k, group).start()
            fin_copy(1, k, group).start()

        @pl.when(group == k)
        def _():
            gk_out[:, pl.ds(gcol, HD)] = final[0, k]
            gv_out[:, pl.ds(gcol, HD)] = final[1, k]

    for level in range(levels):

        @pl.when(ctx + 2**level < n_ctx)
        def _():
            kv_copy(level).wait_send()

        @pl.when(ctx >= 2**level)
        def _():
            ret_copy(level).wait_send()

    for k in range(per_member):
        for off in range(1, repl):
            pair_copy(off, k).wait_send()
    for other in range(n_head):

        @pl.when(head != other)
        def _():
            dq_copy(other, other).wait_send()
            dq_copy(other, other).wait_recv()

    for k in range(kv_heads):

        @pl.when(group != k)
        def _():
            for part in range(2):
                fin_copy(part, k, k).wait_send()
                fin_copy(part, k, k).wait_recv()


def on_device(queries, keys, values, grad_out, block_index):
    shard_rows, q_width = queries.shape
    n_ctx = lax.axis_size("ctx")
    n_head = lax.axis_size("head")
    local_heads = q_width // HD
    kv_heads = keys.shape[1] // HD
    levels = n_ctx.bit_length() - 1
    repl = n_head // kv_heads
    rows_out = shard_rows // n_head
    tiles = shard_rows // BLK
    cols = local_heads * BLK
    pairs = tiles * (tiles + 1) // 2
    sizes = (n_ctx, n_head, kv_heads, local_heads, shard_rows, levels)
    bf16, f32 = jnp.bfloat16, jnp.float32
    vmem = pl.BlockSpec(memory_space=pltpu.VMEM)
    sem = pltpu.SemaphoreType.DMA
    elements = cols * BLK * (pairs + tiles * levels)
    return pl.pallas_call(
        functools.partial(kernel, sizes),
        out_shape=(
            jax.ShapeDtypeStruct((rows_out, n_head * q_width), bf16),
            jax.ShapeDtypeStruct((rows_out, kv_heads * HD), bf16),
            jax.ShapeDtypeStruct((rows_out, kv_heads * HD), bf16),
        ),
        in_specs=[vmem] * 4 + [pl.BlockSpec(memory_space=pltpu.SMEM)],
        out_specs=(vmem,) * 3,
        scratch_shapes=[
            pltpu.VMEM((shard_rows, 2 * HD), bf16),
            pltpu.VMEM((HD, shard_rows), bf16),
            pltpu.VMEM((HD, levels * BLK), bf16),
            pltpu.VMEM((levels, BLK, 2 * HD), bf16),
            pltpu.VMEM((levels, BLK, 2 * HD), bf16),
            pltpu.VMEM((pairs, BLK, cols), f32),
            pltpu.VMEM((pairs, BLK, cols), f32),
            pltpu.VMEM((levels, BLK, cols), f32),
            pltpu.VMEM((levels, BLK, cols), f32),
            pltpu.VMEM((tiles, HD, cols), f32),
            pltpu.VMEM((shard_rows, 2 * HD), f32),
            pltpu.VMEM((levels, BLK, 2 * HD), f32),
            pltpu.VMEM((levels, BLK, 2 * HD), bf16),
            pltpu.VMEM((levels, BLK, 2 * HD), bf16),
            pltpu.VMEM((shard_rows, q_width), bf16),
            pltpu.VMEM((max(repl - 1, 1), kv_heads, rows_out, 2 * HD), bf16),
            pltpu.VMEM((max(repl - 1, 1), kv_heads, rows_out, 2 * HD), bf16),
            pltpu.VMEM((2, kv_heads, rows_out, HD), bf16),
            sem((levels,)),
            sem((levels,)),
            sem((levels,)),
            sem((levels,)),
            sem((n_head,)),
            sem((n_head,)),
            sem((max(repl - 1, 1), kv_heads)),
            sem((max(repl - 1, 1), kv_heads)),
            sem((2, kv_heads)),
            sem((2, kv_heads)),
        ],
        compiler_params=pltpu.CompilerParams(
            collective_id=0, has_side_effects=True, vmem_limit_bytes=48 * 2**20
        ),
        cost_estimate=pl.CostEstimate(
            flops=10 * elements * HD, bytes_accessed=4 * 2**20, transcendentals=elements
        ),
    )(queries, grad_out, keys, values, block_index)


def solution(mesh):
    placed = (P("ctx", "head"), P("ctx", None), P("ctx", None), P("ctx", "head"), P())
    return jax.shard_map(
        on_device,
        mesh=mesh,
        in_specs=placed,
        out_specs=(P(("ctx", "head"), None), P(("ctx", "head"), None), P(("ctx", "head"), None)),
        check_vma=False,
    )
```

```python
import functools

import jax
import jax.numpy as jnp
from jax import lax
from jax.experimental import pallas as pl
from jax.experimental.pallas import tpu as pltpu
from jax.sharding import PartitionSpec as P

HD = 128
BLK = 256
VMEM_LIMIT = 60 * 2**20
LOG2E = 1.4426950408889634
MESH = pl.DeviceIdType.MESH
NT = (((1,), (1,)), ((), ()))
NN = (((1,), (0,)), ((), ()))


def dot(a, b, dims=NN):
    return lax.dot_general(a, b, dims, preferred_element_type=jnp.float32)


def kernel(
    sizes,
    q_hbm,
    do_hbm,
    k_hbm,
    v_hbm,
    index_hbm,
    dq_out,
    gk_out,
    gv_out,
    q_ref,
    do_ref,
    index_ref,
    in_sem,
    own_kv,
    own_kt,
    part_kt,
    kv_send,
    kv_recv,
    w_own,
    dp_own,
    w_part,
    dp_part,
    dq_part,
    acc,
    acc_part,
    ret_send,
    ret_recv,
    dq_stage,
    pair_send,
    pair_recv,
    final,
    kv_ssem,
    kv_rsem,
    ret_ssem,
    ret_rsem,
    dq_ssem,
    dq_rsem,
    pair_ssem,
    pair_rsem,
    fin_ssem,
    fin_rsem,
):
    n_ctx, n_head, kv_heads, local_heads, shard_rows, levels = sizes
    repl = n_head // kv_heads
    per_member = n_head // repl
    rows_out = shard_rows // n_head
    tiles = shard_rows // BLK
    cols = local_heads * BLK
    width = local_heads * HD
    scale = HD ** (-0.5)
    c2 = scale * LOG2E
    ctx = lax.axis_index("ctx")
    head = lax.axis_index("head")
    group = head // repl
    member = head % repl
    gcol = pl.multiple_of(group * HD, HD)

    loads = [
        pltpu.make_async_copy(src, dst, in_sem.at[number])
        for number, (src, dst) in enumerate(
            (
                (k_hbm.at[:, pl.ds(gcol, HD)], own_kv.at[:, :HD]),
                (v_hbm.at[:, pl.ds(gcol, HD)], own_kv.at[:, HD:]),
                (index_hbm, index_ref),
                (q_hbm, q_ref),
                (do_hbm, do_ref),
            )
        )
    ]
    for load in loads:
        load.start()

    barrier = pltpu.get_barrier_semaphore()
    greet = n_head - 1
    for level in range(levels):
        step = 2**level

        @pl.when(ctx + step < n_ctx)
        def _():
            pl.semaphore_signal(barrier, inc=1, device_id=(ctx + step, head), device_id_type=MESH)

        @pl.when(ctx >= step)
        def _():
            pl.semaphore_signal(barrier, inc=1, device_id=(ctx - step, head), device_id_type=MESH)

        greet = greet + jnp.where(ctx + step < n_ctx, 1, 0) + jnp.where(ctx >= step, 1, 0)
    for off in range(1, n_head):
        pl.semaphore_signal(
            barrier, inc=1, device_id=(ctx, (head + off) % n_head), device_id_type=MESH
        )

    for load in loads[:3]:
        load.wait()
    blocks = []

    def is_block(level, block):
        return (blocks[level] == block).astype(jnp.float32)

    for level in range(levels):
        target = jnp.minimum(ctx + 2**level, n_ctx - 1)
        blocks.append(index_ref[level, target])
        chosen = jnp.zeros((BLK, 2 * HD), jnp.float32)
        for block in range(tiles):
            piece = own_kv[block * BLK : (block + 1) * BLK, :].astype(jnp.float32)
            chosen = chosen + piece * is_block(level, block)
        kv_send[level] = chosen.astype(jnp.bfloat16)

    pl.semaphore_wait(barrier, greet)

    def kv_copy(level):
        return pltpu.make_async_remote_copy(
            src_ref=kv_send.at[level],
            dst_ref=kv_recv.at[level],
            send_sem=kv_ssem.at[level],
            recv_sem=kv_rsem.at[level],
            device_id=(jnp.minimum(ctx + 2**level, n_ctx - 1), head),
            device_id_type=MESH,
        )

    for level in reversed(range(levels)):

        @pl.when(ctx + 2**level < n_ctx)
        def _():
            kv_copy(level).start()

        @pl.when(ctx < 2**level)
        def _():
            kv_recv[level] = jnp.zeros((BLK, 2 * HD), jnp.bfloat16)

        @pl.when(ctx + 2**level >= n_ctx)
        def _():
            ret_recv[level] = jnp.zeros((BLK, 2 * HD), jnp.bfloat16)

    def stacked(ref, tile):
        rows = pl.ds(tile * BLK, BLK)
        return jnp.concatenate(
            [ref[rows, h * HD : (h + 1) * HD] for h in range(local_heads)], axis=0
        )

    def slot(tile, block):
        return tile * (tile + 1) // 2 + block

    order = []
    for tile in range((tiles + 1) // 2):
        order += [tiles - 1 - tile] + ([tile] if tile != tiles - 1 - tile else [])
    early = len(order) // 2
    key_pos = lax.broadcasted_iota(jnp.int32, (BLK, cols), 0)
    query_pos = lax.broadcasted_iota(jnp.int32, (BLK, cols), 1) % BLK
    for load in loads[3:]:
        load.wait()
    for block in range(tiles):
        rows = pl.ds(block * BLK, BLK)
        own_kt[:, rows] = own_kv[rows, :HD].T

    own_stats = {}
    for tile in order:
        q_cat, do_cat = stacked(q_ref, tile), stacked(do_ref, tile)
        top = None
        for block in range(tile + 1):
            s = dot(own_kv[block * BLK : (block + 1) * BLK, :HD], q_cat, NT)
            if block == tile:
                s = jnp.where(key_pos <= query_pos, s, -1e30)
            w_own[slot(tile, block)] = s
            high = jnp.max(s, axis=0, keepdims=True)
            top = high if top is None else jnp.maximum(top, high)
        top = top * c2
        total = jnp.zeros((1, cols), jnp.float32)
        mixed = jnp.zeros((1, cols), jnp.float32)
        for block in range(tile + 1):
            w = jnp.exp2(w_own[slot(tile, block)] * c2 - top)
            dp = dot(own_kv[block * BLK : (block + 1) * BLK, HD:], do_cat, NT)
            w_own[slot(tile, block)] = w
            dp_own[slot(tile, block)] = dp
            total = total + jnp.sum(w, axis=0, keepdims=True)
            mixed = mixed + jnp.sum(w * dp, axis=0, keepdims=True)
        own_stats[tile] = (top, total, mixed)

    for level in range(levels):

        @pl.when(ctx >= 2**level)
        def _():
            kv_copy(level).wait_recv()

    dead = []
    for level in range(levels):
        part_kt[:, level * BLK : (level + 1) * BLK] = kv_recv[level, :, :HD].T
        dead.append(jnp.where(ctx >= 2**level, 0.0, 1e30).astype(jnp.float32))

    final_stats = {}

    def partner_part(tile):
        q_cat, do_cat = stacked(q_ref, tile), stacked(do_ref, tile)
        top_own, total_own, mixed_own = own_stats[tile]
        top = top_own
        for level in range(levels):
            s = dot(kv_recv[level, :, :HD], q_cat, NT)
            w_part[level] = s
            top = jnp.maximum(top, jnp.max(s, axis=0, keepdims=True) * c2 - dead[level])
        keep = jnp.exp2(top_own - top)
        total = total_own * keep
        mixed = mixed_own * keep
        for level in range(levels):
            w = jnp.exp2(w_part[level] * c2 - (top + dead[level]))
            dp = dot(kv_recv[level, :, HD:], do_cat, NT)
            w_part[level] = w
            dp_part[level] = dp
            total = total + jnp.sum(w, axis=0, keepdims=True)
            mixed = mixed + jnp.sum(w * dp, axis=0, keepdims=True)
        inverse = 1.0 / total
        delta = mixed * inverse
        final_stats[tile] = (keep * inverse, delta)
        dq_t = None
        for level in range(levels):
            p = w_part[level] * inverse
            ds = (p * (dp_part[level] - delta)).astype(jnp.bfloat16)
            d_value = dot(p.astype(jnp.bfloat16), do_cat)
            d_key = dot(ds, q_cat) * scale
            if tile == order[0]:
                acc_part[level, :, :HD] = d_key
                acc_part[level, :, HD:] = d_value
            else:
                acc_part[level, :, :HD] += d_key
                acc_part[level, :, HD:] += d_value
            piece = dot(part_kt[:, level * BLK : (level + 1) * BLK], ds)
            dq_t = piece if dq_t is None else dq_t + piece
        dq_part[tile] = dq_t

    def send_partner():
        for level in reversed(range(levels)):
            ret_send[level] = acc_part[level].astype(jnp.bfloat16)

            @pl.when(ctx >= 2**level)
            def _():
                ret_copy(level).start()

    def ret_copy(level):
        return pltpu.make_async_remote_copy(
            src_ref=ret_send.at[level],
            dst_ref=ret_recv.at[level],
            send_sem=ret_ssem.at[level],
            recv_sem=ret_rsem.at[level],
            device_id=(jnp.maximum(ctx - 2**level, 0), head),
            device_id_type=MESH,
        )

    def dq_copy(dest, source):
        return pltpu.make_async_remote_copy(
            src_ref=dq_stage.at[pl.ds(dest * rows_out, rows_out), :],
            dst_ref=dq_out.at[:, pl.ds(pl.multiple_of(source * width, width), width)],
            send_sem=dq_ssem.at[dest],
            recv_sem=dq_rsem.at[source],
            device_id=(ctx, dest),
            device_id_type=MESH,
        )

    def dq_keep(dest):
        return pltpu.make_async_copy(
            dq_stage.at[pl.ds(dest * rows_out, rows_out), :],
            dq_out.at[:, pl.ds(pl.multiple_of(head * width, width), width)],
            dq_ssem.at[dest],
        )

    def own_part(tile):
        q_cat, do_cat = stacked(q_ref, tile), stacked(do_ref, tile)
        inverse, delta = final_stats[tile]
        dq_t = dq_part[tile]
        for block in range(tile + 1):
            p = w_own[slot(tile, block)] * inverse
            ds = (p * (dp_own[slot(tile, block)] - delta)).astype(jnp.bfloat16)
            d_value = dot(p.astype(jnp.bfloat16), do_cat)
            d_key = dot(ds, q_cat) * scale
            rows = slice(block * BLK, (block + 1) * BLK)
            if tile == order[0]:
                acc[rows, :HD] = d_key
                acc[rows, HD:] = d_value
            else:
                acc[rows, :HD] += d_key
                acc[rows, HD:] += d_value
            dq_t = dq_t + dot(own_kt[:, rows], ds)
        dq_t = dq_t * scale
        for h in range(local_heads):
            dq_stage[tile * BLK : (tile + 1) * BLK, h * HD : (h + 1) * HD] = (
                dq_t[:, h * BLK : (h + 1) * BLK].T.astype(jnp.bfloat16)
            )
        for dest in range(tile * BLK // rows_out, (tile + 1) * BLK // rows_out):

            @pl.when(head != dest)
            def _():
                dq_copy(dest, head).start()

            @pl.when(head == dest)
            def _():
                dq_keep(dest).start()

    for tile in order[:early]:
        partner_part(tile)
        own_part(tile)
    for tile in order[early:]:
        partner_part(tile)
    send_partner()
    for tile in order[early:]:
        own_part(tile)

    for level in range(levels):

        @pl.when(ctx + 2**level < n_ctx)
        def _():
            ret_copy(level).wait_recv()

    for block in range(tiles):
        rows = slice(block * BLK, (block + 1) * BLK)
        value = acc[rows, :]
        for level in range(levels):
            back = ret_recv[level].astype(jnp.float32)
            value = value + back * is_block(level, block)
        acc[rows, :] = value

    def pair_copy(off, k):
        return pltpu.make_async_remote_copy(
            src_ref=pair_send.at[off - 1, k],
            dst_ref=pair_recv.at[off - 1, k],
            send_sem=pair_ssem.at[off - 1, k],
            recv_sem=pair_rsem.at[off - 1, k],
            device_id=(ctx, group * repl + (member + off) % repl),
            device_id_type=MESH,
        )

    for k in range(per_member):
        for off in range(1, repl):
            begin = pl.multiple_of((k * repl + (member + off) % repl) * rows_out, rows_out)
            pair_send[off - 1, k] = acc[pl.ds(begin, rows_out), :].astype(jnp.bfloat16)
            pair_copy(off, k).start()

    def fin_copy(part, k, source_group):
        out = (gk_out, gv_out)[part]
        return pltpu.make_async_remote_copy(
            src_ref=final.at[part, k],
            dst_ref=out.at[:, pl.ds(pl.multiple_of(source_group * HD, HD), HD)],
            send_sem=fin_ssem.at[part, k],
            recv_sem=fin_rsem.at[part, source_group],
            device_id=(ctx, k * repl + member),
            device_id_type=MESH,
        )

    def fin_keep(part, k):
        out = (gk_out, gv_out)[part]
        return pltpu.make_async_copy(
            final.at[part, k], out.at[:, pl.ds(gcol, HD)], fin_ssem.at[part, k]
        )

    for k in range(per_member):
        begin = pl.multiple_of((k * repl + member) * rows_out, rows_out)
        value = acc[pl.ds(begin, rows_out), :]
        for off in range(1, repl):
            pair_copy(off, k).wait_recv()
            value = value + pair_recv[off - 1, k].astype(jnp.float32)
        final[0, k] = value[:, :HD].astype(jnp.bfloat16)
        final[1, k] = value[:, HD:].astype(jnp.bfloat16)

        @pl.when(group != k)
        def _():
            fin_copy(0, k, group).start()
            fin_copy(1, k, group).start()

        @pl.when(group == k)
        def _():
            fin_keep(0, k).start()
            fin_keep(1, k).start()

    for level in range(levels):

        @pl.when(ctx + 2**level < n_ctx)
        def _():
            kv_copy(level).wait_send()

        @pl.when(ctx >= 2**level)
        def _():
            ret_copy(level).wait_send()

    for k in range(per_member):
        for off in range(1, repl):
            pair_copy(off, k).wait_send()
    for other in range(n_head):

        @pl.when(head != other)
        def _():
            dq_copy(other, other).wait_send()
            dq_copy(other, other).wait_recv()

        @pl.when(head == other)
        def _():
            dq_keep(other).wait()

    for k in range(kv_heads):

        @pl.when(group != k)
        def _():
            for part in range(2):
                fin_copy(part, k, k).wait_send()
                fin_copy(part, k, k).wait_recv()

        @pl.when(group == k)
        def _():
            for part in range(2):
                fin_keep(part, k).wait()


def hand_over(a_in, b_in, c_in, a_out, b_out, c_out, sems):
    copies = [
        pltpu.make_async_copy(src, dst, sems.at[number])
        for number, (src, dst) in enumerate(((a_in, a_out), (b_in, b_out), (c_in, c_out)))
    ]
    for copy in copies:
        copy.start()
    for copy in copies:
        copy.wait()


def on_device(queries, keys, values, grad_out, block_index):
    shard_rows, q_width = queries.shape
    n_ctx = lax.axis_size("ctx")
    n_head = lax.axis_size("head")
    local_heads = q_width // HD
    kv_heads = keys.shape[1] // HD
    levels = n_ctx.bit_length() - 1
    repl = n_head // kv_heads
    rows_out = shard_rows // n_head
    tiles = shard_rows // BLK
    cols = local_heads * BLK
    pairs = tiles * (tiles + 1) // 2
    sizes = (n_ctx, n_head, kv_heads, local_heads, shard_rows, levels)
    bf16, f32 = jnp.bfloat16, jnp.float32
    hbm = pl.BlockSpec(memory_space=pltpu.HBM)
    sem = pltpu.SemaphoreType.DMA
    elements = cols * BLK * (pairs + tiles * levels)
    results = pl.pallas_call(
        functools.partial(kernel, sizes),
        out_shape=(
            jax.ShapeDtypeStruct((rows_out, n_head * q_width), bf16),
            jax.ShapeDtypeStruct((rows_out, kv_heads * HD), bf16),
            jax.ShapeDtypeStruct((rows_out, kv_heads * HD), bf16),
        ),
        in_specs=[hbm] * 5,
        out_specs=(hbm,) * 3,
        scratch_shapes=[
            pltpu.VMEM((shard_rows, q_width), bf16),
            pltpu.VMEM((shard_rows, q_width), bf16),
            pltpu.SMEM((levels, n_ctx), jnp.int32),
            sem((5,)),
            pltpu.VMEM((shard_rows, 2 * HD), bf16),
            pltpu.VMEM((HD, shard_rows), bf16),
            pltpu.VMEM((HD, levels * BLK), bf16),
            pltpu.VMEM((levels, BLK, 2 * HD), bf16),
            pltpu.VMEM((levels, BLK, 2 * HD), bf16),
            pltpu.VMEM((pairs, BLK, cols), f32),
            pltpu.VMEM((pairs, BLK, cols), f32),
            pltpu.VMEM((levels, BLK, cols), f32),
            pltpu.VMEM((levels, BLK, cols), f32),
            pltpu.VMEM((tiles, HD, cols), f32),
            pltpu.VMEM((shard_rows, 2 * HD), f32),
            pltpu.VMEM((levels, BLK, 2 * HD), f32),
            pltpu.VMEM((levels, BLK, 2 * HD), bf16),
            pltpu.VMEM((levels, BLK, 2 * HD), bf16),
            pltpu.VMEM((shard_rows, q_width), bf16),
            pltpu.VMEM((max(repl - 1, 1), kv_heads, rows_out, 2 * HD), bf16),
            pltpu.VMEM((max(repl - 1, 1), kv_heads, rows_out, 2 * HD), bf16),
            pltpu.VMEM((2, kv_heads, rows_out, HD), bf16),
            sem((levels,)),
            sem((levels,)),
            sem((levels,)),
            sem((levels,)),
            sem((n_head,)),
            sem((n_head,)),
            sem((max(repl - 1, 1), kv_heads)),
            sem((max(repl - 1, 1), kv_heads)),
            sem((2, kv_heads)),
            sem((2, kv_heads)),
        ],
        compiler_params=pltpu.CompilerParams(
            collective_id=0, has_side_effects=True, vmem_limit_bytes=VMEM_LIMIT
        ),
        cost_estimate=pl.CostEstimate(
            flops=10 * elements * HD, bytes_accessed=4 * 2**20, transcendentals=elements
        ),
    )(queries, grad_out, keys, values, block_index.T)
    return pl.pallas_call(
        hand_over,
        out_shape=tuple(jax.ShapeDtypeStruct(x.shape, x.dtype) for x in results),
        in_specs=[hbm] * 3,
        out_specs=(hbm,) * 3,
        scratch_shapes=[sem((3,))],
        compiler_params=pltpu.CompilerParams(vmem_limit_bytes=VMEM_LIMIT),
    )(*results)


def solution(mesh):
    placed = (P("ctx", "head"), P("ctx", None), P("ctx", None), P("ctx", "head"), P())
    return jax.shard_map(
        on_device,
        mesh=mesh,
        in_specs=placed,
        out_specs=(P(("ctx", "head"), None), P(("ctx", "head"), None), P(("ctx", "head"), None)),
        check_vma=False,
    )
```

```python
import functools

import jax
import jax.numpy as jnp
from jax import lax
from jax.experimental import pallas as pl
from jax.experimental.pallas import tpu as pltpu
from jax.sharding import PartitionSpec as P

HD = 128
BLK = 256
VMEM_LIMIT = 60 * 2**20
LOG2E = 1.4426950408889634
MESH = pl.DeviceIdType.MESH

def dot(a, b):
    return jnp.dot(a, b, preferred_element_type=jnp.float32)


def kernel(
    sizes,
    q_hbm,
    do_hbm,
    k_hbm,
    v_hbm,
    index_hbm,
    dq_out,
    gk_out,
    gv_out,
    q_ref,
    do_ref,
    index_ref,
    in_sem,
    q_t,
    do_t,
    own_kv,
    own_kt,
    part_kt,
    kv_send,
    kv_recv,
    s_tile,
    w_own,
    dp_own,
    w_part,
    dp_part,
    dq_part,
    acc,
    acc_part,
    ret_send,
    ret_recv,
    dq_stage,
    pair_send,
    pair_recv,
    final,
    kv_ssem,
    kv_rsem,
    ret_ssem,
    ret_rsem,
    dq_ssem,
    dq_rsem,
    pair_ssem,
    pair_rsem,
    fin_ssem,
    fin_rsem,
):
    n_ctx, n_head, kv_heads, local_heads, shard_rows, levels = sizes
    repl = n_head // kv_heads
    per_member = n_head // repl
    rows_out = shard_rows // n_head
    tiles = shard_rows // BLK
    cols = local_heads * BLK
    width = local_heads * HD
    scale = HD ** (-0.5)
    c2 = scale * LOG2E
    ctx = lax.axis_index("ctx")
    head = lax.axis_index("head")
    group = head // repl
    member = head % repl
    gcol = pl.multiple_of(group * HD, HD)

    loads = [
        pltpu.make_async_copy(src, dst, in_sem.at[number])
        for number, (src, dst) in enumerate(
            (
                (k_hbm.at[:, pl.ds(gcol, HD)], own_kv.at[:, :HD]),
                (v_hbm.at[:, pl.ds(gcol, HD)], own_kv.at[:, HD:]),
                (index_hbm, index_ref),
                (q_hbm, q_ref),
                (do_hbm, do_ref),
            )
        )
    ]
    for load in loads:
        load.start()

    barrier = pltpu.get_barrier_semaphore()
    greet = n_head - 1
    for level in range(levels):
        step = 2**level

        @pl.when(ctx + step < n_ctx)
        def _():
            pl.semaphore_signal(barrier, inc=1, device_id=(ctx + step, head), device_id_type=MESH)

        @pl.when(ctx >= step)
        def _():
            pl.semaphore_signal(barrier, inc=1, device_id=(ctx - step, head), device_id_type=MESH)

        greet = greet + jnp.where(ctx + step < n_ctx, 1, 0) + jnp.where(ctx >= step, 1, 0)
    for off in range(1, n_head):
        pl.semaphore_signal(
            barrier, inc=1, device_id=(ctx, (head + off) % n_head), device_id_type=MESH
        )

    for load in loads[:3]:
        load.wait()
    blocks = []

    def is_block(level, block):
        return (blocks[level] == block).astype(jnp.float32)

    for level in range(levels):
        target = jnp.minimum(ctx + 2**level, n_ctx - 1)
        blocks.append(index_ref[level, target])
        chosen = jnp.zeros((BLK, 2 * HD), jnp.float32)
        for block in range(tiles):
            piece = own_kv[block * BLK : (block + 1) * BLK, :].astype(jnp.float32)
            chosen = chosen + piece * is_block(level, block)
        kv_send[level] = chosen.astype(jnp.bfloat16)

    pl.semaphore_wait(barrier, greet)

    def kv_copy(level):
        return pltpu.make_async_remote_copy(
            src_ref=kv_send.at[level],
            dst_ref=kv_recv.at[level],
            send_sem=kv_ssem.at[level],
            recv_sem=kv_rsem.at[level],
            device_id=(jnp.minimum(ctx + 2**level, n_ctx - 1), head),
            device_id_type=MESH,
        )

    for level in reversed(range(levels)):

        @pl.when(ctx + 2**level < n_ctx)
        def _():
            kv_copy(level).start()

        @pl.when(ctx < 2**level)
        def _():
            kv_recv[level] = jnp.zeros((BLK, 2 * HD), jnp.bfloat16)

        @pl.when(ctx + 2**level >= n_ctx)
        def _():
            ret_recv[level] = jnp.zeros((BLK, 2 * HD), jnp.bfloat16)

    def stacked(ref, tile):
        rows = pl.ds(tile * BLK, BLK)
        return jnp.concatenate(
            [ref[rows, h * HD : (h + 1) * HD] for h in range(local_heads)], axis=0
        )

    def slot(tile, block):
        return tile * (tile + 1) // 2 + block

    order = []
    for tile in range((tiles + 1) // 2):
        order += [tiles - 1 - tile] + ([tile] if tile != tiles - 1 - tile else [])
    early = len(order) // 2
    key_pos = lax.broadcasted_iota(jnp.int32, (BLK, cols), 0)
    query_pos = lax.broadcasted_iota(jnp.int32, (BLK, cols), 1) % BLK
    for load in loads[3:]:
        load.wait()
    for block in range(tiles):
        rows = pl.ds(block * BLK, BLK)
        own_kt[:, rows] = own_kv[rows, :HD].T

    own_stats = {}
    for tile in order:
        q_t[tile] = stacked(q_ref, tile).T
        do_t[tile] = stacked(do_ref, tile).T
    for tile in order:
        q_cat, do_cat = stacked(q_ref, tile), stacked(do_ref, tile)
        top = None
        for block in range(tile + 1):
            s = dot(own_kv[block * BLK : (block + 1) * BLK, :HD], q_t[tile])
            if block == tile:
                s = jnp.where(key_pos <= query_pos, s, -1e30)
            s_tile[block] = s
            high = jnp.max(s, axis=0, keepdims=True)
            top = high if top is None else jnp.maximum(top, high)
        top = top * c2
        total = jnp.zeros((1, cols), jnp.float32)
        mixed = jnp.zeros((1, cols), jnp.float32)
        for block in range(tile + 1):
            w = jnp.exp2(s_tile[block] * c2 - top)
            dp = dot(own_kv[block * BLK : (block + 1) * BLK, HD:], do_t[tile])
            w_own[slot(tile, block)] = w.astype(jnp.bfloat16)
            dp_own[slot(tile, block)] = dp
            total = total + jnp.sum(w, axis=0, keepdims=True)
            mixed = mixed + jnp.sum(w * dp, axis=0, keepdims=True)
        own_stats[tile] = (top, total, mixed)

    for level in range(levels):

        @pl.when(ctx >= 2**level)
        def _():
            kv_copy(level).wait_recv()

    dead = []
    for level in range(levels):
        part_kt[:, level * BLK : (level + 1) * BLK] = kv_recv[level, :, :HD].T
        dead.append(jnp.where(ctx >= 2**level, 0.0, 1e30).astype(jnp.float32))

    final_stats = {}

    def partner_part(tile):
        q_cat, do_cat = stacked(q_ref, tile), stacked(do_ref, tile)
        top_own, total_own, mixed_own = own_stats[tile]
        top = top_own
        for level in range(levels):
            s = dot(kv_recv[level, :, :HD], q_t[tile])
            s_tile[level] = s
            top = jnp.maximum(top, jnp.max(s, axis=0, keepdims=True) * c2 - dead[level])
        keep = jnp.exp2(top_own - top)
        total = total_own * keep
        mixed = mixed_own * keep
        for level in range(levels):
            w = jnp.exp2(s_tile[level] * c2 - (top + dead[level]))
            dp = dot(kv_recv[level, :, HD:], do_t[tile])
            w_part[level] = w.astype(jnp.bfloat16)
            dp_part[level] = dp
            total = total + jnp.sum(w, axis=0, keepdims=True)
            mixed = mixed + jnp.sum(w * dp, axis=0, keepdims=True)
        inverse = 1.0 / total
        delta = mixed * inverse
        inverse_low = inverse.astype(jnp.bfloat16)
        final_stats[tile] = ((keep * inverse).astype(jnp.bfloat16), delta)
        dq_t = None
        for level in range(levels):
            p = w_part[level] * inverse_low
            ds = p * (dp_part[level] - delta).astype(jnp.bfloat16)
            d_value = dot(p, do_cat)
            d_key = dot(ds, q_cat)
            if tile == order[0]:
                acc_part[level, :, :HD] = d_key
                acc_part[level, :, HD:] = d_value
            else:
                acc_part[level, :, :HD] += d_key
                acc_part[level, :, HD:] += d_value
            piece = dot(part_kt[:, level * BLK : (level + 1) * BLK], ds)
            dq_t = piece if dq_t is None else dq_t + piece
        dq_part[tile] = dq_t

    def send_partner():
        for level in reversed(range(levels)):
            ret_send[level, :, :HD] = (acc_part[level, :, :HD] * scale).astype(jnp.bfloat16)
            ret_send[level, :, HD:] = acc_part[level, :, HD:].astype(jnp.bfloat16)

            @pl.when(ctx >= 2**level)
            def _():
                ret_copy(level).start()

    def ret_copy(level):
        return pltpu.make_async_remote_copy(
            src_ref=ret_send.at[level],
            dst_ref=ret_recv.at[level],
            send_sem=ret_ssem.at[level],
            recv_sem=ret_rsem.at[level],
            device_id=(jnp.maximum(ctx - 2**level, 0), head),
            device_id_type=MESH,
        )

    def dq_copy(dest, source):
        return pltpu.make_async_remote_copy(
            src_ref=dq_stage.at[pl.ds(dest * rows_out, rows_out), :],
            dst_ref=dq_out.at[:, pl.ds(pl.multiple_of(source * width, width), width)],
            send_sem=dq_ssem.at[dest],
            recv_sem=dq_rsem.at[source],
            device_id=(ctx, dest),
            device_id_type=MESH,
        )

    def dq_keep(dest):
        return pltpu.make_async_copy(
            dq_stage.at[pl.ds(dest * rows_out, rows_out), :],
            dq_out.at[:, pl.ds(pl.multiple_of(head * width, width), width)],
            dq_ssem.at[dest],
        )

    def own_part(tile):
        q_cat, do_cat = stacked(q_ref, tile), stacked(do_ref, tile)
        inverse_low, delta = final_stats[tile]
        dq_t = dq_part[tile]
        for block in range(tile + 1):
            p = w_own[slot(tile, block)] * inverse_low
            ds = p * (dp_own[slot(tile, block)] - delta).astype(jnp.bfloat16)
            d_value = dot(p, do_cat)
            d_key = dot(ds, q_cat)
            rows = slice(block * BLK, (block + 1) * BLK)
            if tile == order[0]:
                acc[rows, :HD] = d_key
                acc[rows, HD:] = d_value
            else:
                acc[rows, :HD] += d_key
                acc[rows, HD:] += d_value
            dq_t = dq_t + dot(own_kt[:, rows], ds)
        dq_t = dq_t * scale
        for h in range(local_heads):
            dq_stage[tile * BLK : (tile + 1) * BLK, h * HD : (h + 1) * HD] = (
                dq_t[:, h * BLK : (h + 1) * BLK].T.astype(jnp.bfloat16)
            )
        for dest in range(tile * BLK // rows_out, (tile + 1) * BLK // rows_out):

            @pl.when(head != dest)
            def _():
                dq_copy(dest, head).start()

            @pl.when(head == dest)
            def _():
                dq_keep(dest).start()

    for tile in order[:early]:
        partner_part(tile)
        own_part(tile)
    for tile in order[early:]:
        partner_part(tile)
    send_partner()
    for tile in order[early:]:
        own_part(tile)

    for level in range(levels):

        @pl.when(ctx + 2**level < n_ctx)
        def _():
            ret_copy(level).wait_recv()

    for block in range(tiles):
        rows = slice(block * BLK, (block + 1) * BLK)
        value = jnp.concatenate([acc[rows, :HD] * scale, acc[rows, HD:]], axis=1)
        for level in range(levels):
            back = ret_recv[level].astype(jnp.float32)
            value = value + back * is_block(level, block)
        acc[rows, :] = value

    def pair_copy(off, k):
        return pltpu.make_async_remote_copy(
            src_ref=pair_send.at[off - 1, k],
            dst_ref=pair_recv.at[off - 1, k],
            send_sem=pair_ssem.at[off - 1, k],
            recv_sem=pair_rsem.at[off - 1, k],
            device_id=(ctx, group * repl + (member + off) % repl),
            device_id_type=MESH,
        )

    for k in range(per_member):
        for off in range(1, repl):
            begin = pl.multiple_of((k * repl + (member + off) % repl) * rows_out, rows_out)
            pair_send[off - 1, k] = acc[pl.ds(begin, rows_out), :].astype(jnp.bfloat16)
            pair_copy(off, k).start()

    def fin_copy(part, k, source_group):
        out = (gk_out, gv_out)[part]
        return pltpu.make_async_remote_copy(
            src_ref=final.at[part, k],
            dst_ref=out.at[:, pl.ds(pl.multiple_of(source_group * HD, HD), HD)],
            send_sem=fin_ssem.at[part, k],
            recv_sem=fin_rsem.at[part, source_group],
            device_id=(ctx, k * repl + member),
            device_id_type=MESH,
        )

    def fin_keep(part, k):
        out = (gk_out, gv_out)[part]
        return pltpu.make_async_copy(
            final.at[part, k], out.at[:, pl.ds(gcol, HD)], fin_ssem.at[part, k]
        )

    for k in range(per_member):
        begin = pl.multiple_of((k * repl + member) * rows_out, rows_out)
        value = acc[pl.ds(begin, rows_out), :]
        for off in range(1, repl):
            pair_copy(off, k).wait_recv()
            value = value + pair_recv[off - 1, k].astype(jnp.float32)
        final[0, k] = value[:, :HD].astype(jnp.bfloat16)
        final[1, k] = value[:, HD:].astype(jnp.bfloat16)

        @pl.when(group != k)
        def _():
            fin_copy(0, k, group).start()
            fin_copy(1, k, group).start()

        @pl.when(group == k)
        def _():
            fin_keep(0, k).start()
            fin_keep(1, k).start()

    for level in range(levels):

        @pl.when(ctx + 2**level < n_ctx)
        def _():
            kv_copy(level).wait_send()

        @pl.when(ctx >= 2**level)
        def _():
            ret_copy(level).wait_send()

    for k in range(per_member):
        for off in range(1, repl):
            pair_copy(off, k).wait_send()
    for other in range(n_head):

        @pl.when(head != other)
        def _():
            dq_copy(other, other).wait_send()
            dq_copy(other, other).wait_recv()

        @pl.when(head == other)
        def _():
            dq_keep(other).wait()

    for k in range(kv_heads):

        @pl.when(group != k)
        def _():
            for part in range(2):
                fin_copy(part, k, k).wait_send()
                fin_copy(part, k, k).wait_recv()

        @pl.when(group == k)
        def _():
            for part in range(2):
                fin_keep(part, k).wait()


def hand_over(a_in, b_in, c_in, a_out, b_out, c_out, a_mid, b_mid, c_mid, in_sems, out_sems):
    mids = (a_mid, b_mid, c_mid)
    loads = [
        pltpu.make_async_copy(src, dst, in_sems.at[number])
        for number, (src, dst) in enumerate(zip((a_in, b_in, c_in), mids))
    ]
    stores = [
        pltpu.make_async_copy(src, dst, out_sems.at[number])
        for number, (src, dst) in enumerate(zip(mids, (a_out, b_out, c_out)))
    ]
    for load in loads:
        load.start()
    for load, store in zip(loads, stores):
        load.wait()
        store.start()
    for store in stores:
        store.wait()


def on_device(queries, keys, values, grad_out, block_index):
    shard_rows, q_width = queries.shape
    n_ctx = lax.axis_size("ctx")
    n_head = lax.axis_size("head")
    local_heads = q_width // HD
    kv_heads = keys.shape[1] // HD
    levels = n_ctx.bit_length() - 1
    repl = n_head // kv_heads
    rows_out = shard_rows // n_head
    tiles = shard_rows // BLK
    cols = local_heads * BLK
    pairs = tiles * (tiles + 1) // 2
    sizes = (n_ctx, n_head, kv_heads, local_heads, shard_rows, levels)
    bf16, f32 = jnp.bfloat16, jnp.float32
    hbm = pl.BlockSpec(memory_space=pltpu.HBM)
    sem = pltpu.SemaphoreType.DMA
    elements = cols * BLK * (pairs + tiles * levels)
    results = pl.pallas_call(
        functools.partial(kernel, sizes),
        out_shape=(
            jax.ShapeDtypeStruct((rows_out, n_head * q_width), bf16),
            jax.ShapeDtypeStruct((rows_out, kv_heads * HD), bf16),
            jax.ShapeDtypeStruct((rows_out, kv_heads * HD), bf16),
        ),
        in_specs=[hbm] * 5,
        out_specs=(hbm,) * 3,
        scratch_shapes=[
            pltpu.VMEM((shard_rows, q_width), bf16),
            pltpu.VMEM((shard_rows, q_width), bf16),
            pltpu.SMEM((levels, n_ctx), jnp.int32),
            sem((5,)),
            pltpu.VMEM((tiles, HD, cols), bf16),
            pltpu.VMEM((tiles, HD, cols), bf16),
            pltpu.VMEM((shard_rows, 2 * HD), bf16),
            pltpu.VMEM((HD, shard_rows), bf16),
            pltpu.VMEM((HD, levels * BLK), bf16),
            pltpu.VMEM((levels, BLK, 2 * HD), bf16),
            pltpu.VMEM((levels, BLK, 2 * HD), bf16),
            pltpu.VMEM((max(tiles, levels), BLK, cols), f32),
            pltpu.VMEM((pairs, BLK, cols), bf16),
            pltpu.VMEM((pairs, BLK, cols), f32),
            pltpu.VMEM((levels, BLK, cols), bf16),
            pltpu.VMEM((levels, BLK, cols), f32),
            pltpu.VMEM((tiles, HD, cols), f32),
            pltpu.VMEM((shard_rows, 2 * HD), f32),
            pltpu.VMEM((levels, BLK, 2 * HD), f32),
            pltpu.VMEM((levels, BLK, 2 * HD), bf16),
            pltpu.VMEM((levels, BLK, 2 * HD), bf16),
            pltpu.VMEM((shard_rows, q_width), bf16),
            pltpu.VMEM((max(repl - 1, 1), kv_heads, rows_out, 2 * HD), bf16),
            pltpu.VMEM((max(repl - 1, 1), kv_heads, rows_out, 2 * HD), bf16),
            pltpu.VMEM((2, kv_heads, rows_out, HD), bf16),
            sem((levels,)),
            sem((levels,)),
            sem((levels,)),
            sem((levels,)),
            sem((n_head,)),
            sem((n_head,)),
            sem((max(repl - 1, 1), kv_heads)),
            sem((max(repl - 1, 1), kv_heads)),
            sem((2, kv_heads)),
            sem((2, kv_heads)),
        ],
        compiler_params=pltpu.CompilerParams(
            collective_id=0, has_side_effects=True, vmem_limit_bytes=VMEM_LIMIT
        ),
        cost_estimate=pl.CostEstimate(
            flops=10 * elements * HD, bytes_accessed=4 * 2**20, transcendentals=elements
        ),
    )(queries, grad_out, keys, values, block_index.T)
    return pl.pallas_call(
        hand_over,
        out_shape=tuple(jax.ShapeDtypeStruct(x.shape, x.dtype) for x in results),
        in_specs=[hbm] * 3,
        out_specs=(hbm,) * 3,
        scratch_shapes=[pltpu.VMEM(x.shape, x.dtype) for x in results] + [sem((3,)), sem((3,))],
        compiler_params=pltpu.CompilerParams(vmem_limit_bytes=VMEM_LIMIT),
    )(*results)


def solution(mesh):
    placed = (P("ctx", "head"), P("ctx", None), P("ctx", None), P("ctx", "head"), P())
    return jax.shard_map(
        on_device,
        mesh=mesh,
        in_specs=placed,
        out_specs=(P(("ctx", "head"), None), P(("ctx", "head"), None), P(("ctx", "head"), None)),
        check_vma=False,
    )
```

```python
import functools

import jax
import jax.numpy as jnp
from jax import lax
from jax.experimental import pallas as pl
from jax.experimental.pallas import tpu as pltpu
from jax.sharding import PartitionSpec as P

HD = 128
BLK = 256
VMEM_LIMIT = 60 * 2**20
LOG2E = 1.4426950408889634
MESH = pl.DeviceIdType.MESH

def dot(a, b):
    return jnp.dot(a, b, preferred_element_type=jnp.float32)


def kernel(
    sizes,
    q_hbm,
    do_hbm,
    k_hbm,
    v_hbm,
    index_hbm,
    dq_out,
    gk_out,
    gv_out,
    q_ref,
    do_ref,
    index_ref,
    in_sem,
    q_t,
    do_t,
    own_kv,
    own_kt,
    part_kt,
    kv_send,
    kv_recv,
    s_tile,
    w_own,
    dp_own,
    w_part,
    dp_part,
    dq_part,
    acc,
    acc_part,
    ret_send,
    ret_recv,
    dq_stage,
    part_send,
    part_recv,
    own_send,
    own_recv,
    final,
    kv_ssem,
    kv_rsem,
    ret_ssem,
    ret_rsem,
    dq_ssem,
    dq_rsem,
    part_ssem,
    part_rsem,
    own_ssem,
    own_rsem,
    fin_ssem,
    fin_rsem,
):
    n_ctx, n_head, kv_heads, local_heads, shard_rows, levels = sizes
    repl = n_head // kv_heads
    rows_out = shard_rows // n_head
    tiles = shard_rows // BLK
    cols = local_heads * BLK
    width = local_heads * HD
    scale = HD ** (-0.5)
    c2 = scale * LOG2E
    ctx = lax.axis_index("ctx")
    head = lax.axis_index("head")
    group = head // repl
    member = head % repl
    gcol = pl.multiple_of(group * HD, HD)
    mate = group * repl + (1 - member)
    mcol = pl.multiple_of(member * HD, HD)
    ocol = pl.multiple_of((1 - member) * HD, HD)

    loads = [
        pltpu.make_async_copy(src, dst, in_sem.at[number])
        for number, (src, dst) in enumerate(
            (
                (k_hbm.at[:, pl.ds(gcol, HD)], own_kv.at[:, :HD]),
                (v_hbm.at[:, pl.ds(gcol, HD)], own_kv.at[:, HD:]),
                (index_hbm, index_ref),
                (q_hbm, q_ref),
                (do_hbm, do_ref),
            )
        )
    ]
    for load in loads:
        load.start()

    barrier = pltpu.get_barrier_semaphore()
    greet = n_head - 1
    for level in range(levels):
        step = 2**level

        @pl.when(ctx + step < n_ctx)
        def _():
            pl.semaphore_signal(barrier, inc=1, device_id=(ctx + step, head), device_id_type=MESH)

        @pl.when(ctx >= step)
        def _():
            pl.semaphore_signal(barrier, inc=1, device_id=(ctx - step, head), device_id_type=MESH)

        greet = greet + jnp.where(ctx + step < n_ctx, 1, 0) + jnp.where(ctx >= step, 1, 0)
    for off in range(1, n_head):
        pl.semaphore_signal(
            barrier, inc=1, device_id=(ctx, (head + off) % n_head), device_id_type=MESH
        )

    for load in loads[:3]:
        load.wait()
    blocks = []

    def is_block(level, block):
        return (blocks[level] == block).astype(jnp.float32)

    for level in range(levels):
        target = jnp.minimum(ctx + 2**level, n_ctx - 1)
        blocks.append(index_ref[level, target])
        chosen = jnp.zeros((BLK, 2 * HD), jnp.float32)
        for block in range(tiles):
            piece = own_kv[block * BLK : (block + 1) * BLK, :].astype(jnp.float32)
            chosen = chosen + piece * is_block(level, block)
        kv_send[level] = chosen.astype(jnp.bfloat16)

    pl.semaphore_wait(barrier, greet)

    def kv_copy(level):
        return pltpu.make_async_remote_copy(
            src_ref=kv_send.at[level],
            dst_ref=kv_recv.at[level],
            send_sem=kv_ssem.at[level],
            recv_sem=kv_rsem.at[level],
            device_id=(jnp.minimum(ctx + 2**level, n_ctx - 1), head),
            device_id_type=MESH,
        )

    for level in reversed(range(levels)):

        @pl.when(ctx + 2**level < n_ctx)
        def _():
            kv_copy(level).start()

        @pl.when(ctx < 2**level)
        def _():
            kv_recv[level] = jnp.zeros((BLK, 2 * HD), jnp.bfloat16)

        @pl.when(ctx + 2**level >= n_ctx)
        def _():
            ret_recv[level] = jnp.zeros((BLK, HD), jnp.bfloat16)

    def stacked(ref, tile):
        rows = pl.ds(tile * BLK, BLK)
        return jnp.concatenate(
            [ref[rows, h * HD : (h + 1) * HD] for h in range(local_heads)], axis=0
        )

    def slot(tile, block):
        return tile * (tile + 1) // 2 + block

    order = []
    for tile in range((tiles + 1) // 2):
        order += [tiles - 1 - tile] + ([tile] if tile != tiles - 1 - tile else [])
    early = len(order) // 2
    key_pos = lax.broadcasted_iota(jnp.int32, (BLK, cols), 0)
    query_pos = lax.broadcasted_iota(jnp.int32, (BLK, cols), 1) % BLK
    for load in loads[3:]:
        load.wait()
    for block in range(tiles):
        rows = pl.ds(block * BLK, BLK)
        own_kt[:, rows] = own_kv[rows, :HD].T

    own_stats = {}
    for tile in order:
        q_t[tile] = stacked(q_ref, tile).T
        do_t[tile] = stacked(do_ref, tile).T
    for tile in order:
        q_cat, do_cat = stacked(q_ref, tile), stacked(do_ref, tile)
        top = None
        for block in range(tile + 1):
            s = dot(own_kv[block * BLK : (block + 1) * BLK, :HD], q_t[tile])
            if block == tile:
                s = jnp.where(key_pos <= query_pos, s, -1e30)
            s_tile[block] = s
            high = jnp.max(s, axis=0, keepdims=True)
            top = high if top is None else jnp.maximum(top, high)
        top = top * c2
        total = jnp.zeros((1, cols), jnp.float32)
        mixed = jnp.zeros((1, cols), jnp.float32)
        for block in range(tile + 1):
            w = jnp.exp2(s_tile[block] * c2 - top)
            dp = dot(own_kv[block * BLK : (block + 1) * BLK, HD:], do_t[tile])
            w_own[slot(tile, block)] = w.astype(jnp.bfloat16)
            dp_own[slot(tile, block)] = dp
            total = total + jnp.sum(w, axis=0, keepdims=True)
            mixed = mixed + jnp.sum(w * dp, axis=0, keepdims=True)
        own_stats[tile] = (top, total, mixed)

    for level in range(levels):

        @pl.when(ctx >= 2**level)
        def _():
            kv_copy(level).wait_recv()

    dead = []
    for level in range(levels):
        part_kt[:, level * BLK : (level + 1) * BLK] = kv_recv[level, :, :HD].T
        dead.append(jnp.where(ctx >= 2**level, 0.0, 1e30).astype(jnp.float32))

    final_stats = {}

    def partner_part(tile):
        q_cat, do_cat = stacked(q_ref, tile), stacked(do_ref, tile)
        top_own, total_own, mixed_own = own_stats[tile]
        top = top_own
        for level in range(levels):
            s = dot(kv_recv[level, :, :HD], q_t[tile])
            s_tile[level] = s
            top = jnp.maximum(top, jnp.max(s, axis=0, keepdims=True) * c2 - dead[level])
        keep = jnp.exp2(top_own - top)
        total = total_own * keep
        mixed = mixed_own * keep
        for level in range(levels):
            w = jnp.exp2(s_tile[level] * c2 - (top + dead[level]))
            dp = dot(kv_recv[level, :, HD:], do_t[tile])
            w_part[level] = w.astype(jnp.bfloat16)
            dp_part[level] = dp
            total = total + jnp.sum(w, axis=0, keepdims=True)
            mixed = mixed + jnp.sum(w * dp, axis=0, keepdims=True)
        inverse = 1.0 / total
        delta = mixed * inverse
        inverse_low = inverse.astype(jnp.bfloat16)
        final_stats[tile] = ((keep * inverse).astype(jnp.bfloat16), delta)
        dq_t = None
        for level in range(levels):
            p = w_part[level] * inverse_low
            ds = p * (dp_part[level] - delta).astype(jnp.bfloat16)
            d_value = dot(p, do_cat)
            d_key = dot(ds, q_cat)
            if tile == order[0]:
                acc_part[level, :, :HD] = d_key
                acc_part[level, :, HD:] = d_value
            else:
                acc_part[level, :, :HD] += d_key
                acc_part[level, :, HD:] += d_value
            piece = dot(part_kt[:, level * BLK : (level + 1) * BLK], ds)
            dq_t = piece if dq_t is None else dq_t + piece
        dq_part[tile] = dq_t

    def part_copy(level):
        return pltpu.make_async_remote_copy(
            src_ref=part_send.at[level],
            dst_ref=part_recv.at[level],
            send_sem=part_ssem.at[level],
            recv_sem=part_rsem.at[level],
            device_id=(ctx, mate),
            device_id_type=MESH,
        )

    def own_copy(block):
        return pltpu.make_async_remote_copy(
            src_ref=own_send.at[block],
            dst_ref=own_recv.at[block],
            send_sem=own_ssem.at[block],
            recv_sem=own_rsem.at[block],
            device_id=(ctx, mate),
            device_id_type=MESH,
        )

    def send_partner():
        for level in reversed(range(levels)):

            @pl.when(ctx >= 2**level)
            def _():
                part_send[level] = acc_part[level, :, pl.ds(ocol, HD)].astype(jnp.bfloat16)
                part_copy(level).start()

    def return_partner():
        for level in reversed(range(levels)):

            @pl.when(ctx >= 2**level)
            def _():
                part_copy(level).wait_recv()
                ret_send[level] = (
                    acc_part[level, :, pl.ds(mcol, HD)] + part_recv[level].astype(jnp.float32)
                ).astype(jnp.bfloat16)
                ret_copy(level).start()

    def send_own(block):
        rows = slice(block * BLK, (block + 1) * BLK)
        own_send[block] = acc[rows, pl.ds(ocol, HD)].astype(jnp.bfloat16)
        own_copy(block).start()

    def ret_copy(level):
        return pltpu.make_async_remote_copy(
            src_ref=ret_send.at[level],
            dst_ref=ret_recv.at[level],
            send_sem=ret_ssem.at[level],
            recv_sem=ret_rsem.at[level],
            device_id=(jnp.maximum(ctx - 2**level, 0), head),
            device_id_type=MESH,
        )

    def dq_copy(dest, source):
        return pltpu.make_async_remote_copy(
            src_ref=dq_stage.at[pl.ds(dest * rows_out, rows_out), :],
            dst_ref=dq_out.at[:, pl.ds(pl.multiple_of(source * width, width), width)],
            send_sem=dq_ssem.at[dest],
            recv_sem=dq_rsem.at[source],
            device_id=(ctx, dest),
            device_id_type=MESH,
        )

    def dq_keep(dest):
        return pltpu.make_async_copy(
            dq_stage.at[pl.ds(dest * rows_out, rows_out), :],
            dq_out.at[:, pl.ds(pl.multiple_of(head * width, width), width)],
            dq_ssem.at[dest],
        )

    def own_part(tile):
        q_cat, do_cat = stacked(q_ref, tile), stacked(do_ref, tile)
        inverse_low, delta = final_stats[tile]
        dq_t = dq_part[tile]
        for block in range(tile + 1):
            p = w_own[slot(tile, block)] * inverse_low
            ds = p * (dp_own[slot(tile, block)] - delta).astype(jnp.bfloat16)
            d_value = dot(p, do_cat)
            d_key = dot(ds, q_cat)
            rows = slice(block * BLK, (block + 1) * BLK)
            if tile == order[0]:
                acc[rows, :HD] = d_key
                acc[rows, HD:] = d_value
            else:
                acc[rows, :HD] += d_key
                acc[rows, HD:] += d_value
            dq_t = dq_t + dot(own_kt[:, rows], ds)
        dq_t = dq_t * scale
        for h in range(local_heads):
            dq_stage[tile * BLK : (tile + 1) * BLK, h * HD : (h + 1) * HD] = (
                dq_t[:, h * BLK : (h + 1) * BLK].T.astype(jnp.bfloat16)
            )
        for dest in range(tile * BLK // rows_out, (tile + 1) * BLK // rows_out):

            @pl.when(head != dest)
            def _():
                dq_copy(dest, head).start()

            @pl.when(head == dest)
            def _():
                dq_keep(dest).start()

    last_use = [max(order.index(tile) for tile in range(block, tiles)) for block in range(tiles)]
    for tile in order:
        partner_part(tile)
    send_partner()
    for number, tile in enumerate(order):
        own_part(tile)
        for block in reversed(range(tiles)):
            if last_use[block] == number:
                send_own(block)
        if number == early - 1:
            return_partner()

    for level in range(levels):

        @pl.when(ctx + 2**level < n_ctx)
        def _():
            ret_copy(level).wait_recv()

    factor = jnp.where(member == 0, scale, 1.0).astype(jnp.float32)

    def fin_copy(part, dest, source):
        out = (gk_out, gv_out)[part]
        return pltpu.make_async_remote_copy(
            src_ref=final.at[pl.ds(dest * rows_out, rows_out), :],
            dst_ref=out.at[:, pl.ds(pl.multiple_of(source // repl * HD, HD), HD)],
            send_sem=fin_ssem.at[dest],
            recv_sem=fin_rsem.at[source],
            device_id=(ctx, dest),
            device_id_type=MESH,
        )

    def fin_keep(part, dest):
        out = (gk_out, gv_out)[part]
        return pltpu.make_async_copy(
            final.at[pl.ds(dest * rows_out, rows_out), :],
            out.at[:, pl.ds(gcol, HD)],
            fin_ssem.at[dest],
        )

    for block in reversed(range(tiles)):
        rows = slice(block * BLK, (block + 1) * BLK)
        own_copy(block).wait_recv()
        value = acc[rows, pl.ds(mcol, HD)] + own_recv[block].astype(jnp.float32)
        for level in range(levels):
            value = value + ret_recv[level].astype(jnp.float32) * is_block(level, block)
        final[rows, :] = (value * factor).astype(jnp.bfloat16)
        for dest in range(block * BLK // rows_out, (block + 1) * BLK // rows_out):
            for part in range(2):

                @pl.when((head != dest) & (member == part))
                def _():
                    fin_copy(part, dest, head).start()

                @pl.when((head == dest) & (member == part))
                def _():
                    fin_keep(part, dest).start()

    for level in range(levels):

        @pl.when(ctx + 2**level < n_ctx)
        def _():
            kv_copy(level).wait_send()

        @pl.when(ctx >= 2**level)
        def _():
            ret_copy(level).wait_send()

    for level in range(levels):

        @pl.when(ctx >= 2**level)
        def _():
            part_copy(level).wait_send()

    for block in range(tiles):
        own_copy(block).wait_send()
    for other in range(n_head):

        @pl.when(head != other)
        def _():
            dq_copy(other, other).wait_send()
            dq_copy(other, other).wait_recv()
            fin_copy(0, other, other).wait_send()
            fin_copy(0, other, other).wait_recv()

        @pl.when(head == other)
        def _():
            dq_keep(other).wait()
            fin_keep(0, other).wait()


def hand_over(a_in, b_in, c_in, a_out, b_out, c_out, a_mid, b_mid, c_mid, in_sems, out_sems):
    mids = (a_mid, b_mid, c_mid)
    loads = [
        pltpu.make_async_copy(src, dst, in_sems.at[number])
        for number, (src, dst) in enumerate(zip((a_in, b_in, c_in), mids))
    ]
    stores = [
        pltpu.make_async_copy(src, dst, out_sems.at[number])
        for number, (src, dst) in enumerate(zip(mids, (a_out, b_out, c_out)))
    ]
    for load in loads:
        load.start()
    for load, store in zip(loads, stores):
        load.wait()
        store.start()
    for store in stores:
        store.wait()


def on_device(queries, keys, values, grad_out, block_index):
    shard_rows, q_width = queries.shape
    n_ctx = lax.axis_size("ctx")
    n_head = lax.axis_size("head")
    local_heads = q_width // HD
    kv_heads = keys.shape[1] // HD
    levels = n_ctx.bit_length() - 1
    rows_out = shard_rows // n_head
    tiles = shard_rows // BLK
    cols = local_heads * BLK
    pairs = tiles * (tiles + 1) // 2
    sizes = (n_ctx, n_head, kv_heads, local_heads, shard_rows, levels)
    bf16, f32 = jnp.bfloat16, jnp.float32
    hbm = pl.BlockSpec(memory_space=pltpu.HBM)
    sem = pltpu.SemaphoreType.DMA
    elements = cols * BLK * (pairs + tiles * levels)
    results = pl.pallas_call(
        functools.partial(kernel, sizes),
        out_shape=(
            jax.ShapeDtypeStruct((rows_out, n_head * q_width), bf16),
            jax.ShapeDtypeStruct((rows_out, kv_heads * HD), bf16),
            jax.ShapeDtypeStruct((rows_out, kv_heads * HD), bf16),
        ),
        in_specs=[hbm] * 5,
        out_specs=(hbm,) * 3,
        scratch_shapes=[
            pltpu.VMEM((shard_rows, q_width), bf16),
            pltpu.VMEM((shard_rows, q_width), bf16),
            pltpu.SMEM((levels, n_ctx), jnp.int32),
            sem((5,)),
            pltpu.VMEM((tiles, HD, cols), bf16),
            pltpu.VMEM((tiles, HD, cols), bf16),
            pltpu.VMEM((shard_rows, 2 * HD), bf16),
            pltpu.VMEM((HD, shard_rows), bf16),
            pltpu.VMEM((HD, levels * BLK), bf16),
            pltpu.VMEM((levels, BLK, 2 * HD), bf16),
            pltpu.VMEM((levels, BLK, 2 * HD), bf16),
            pltpu.VMEM((max(tiles, levels), BLK, cols), f32),
            pltpu.VMEM((pairs, BLK, cols), bf16),
            pltpu.VMEM((pairs, BLK, cols), f32),
            pltpu.VMEM((levels, BLK, cols), bf16),
            pltpu.VMEM((levels, BLK, cols), f32),
            pltpu.VMEM((tiles, HD, cols), f32),
            pltpu.VMEM((shard_rows, 2 * HD), f32),
            pltpu.VMEM((levels, BLK, 2 * HD), f32),
            pltpu.VMEM((levels, BLK, HD), bf16),
            pltpu.VMEM((levels, BLK, HD), bf16),
            pltpu.VMEM((shard_rows, q_width), bf16),
            pltpu.VMEM((levels, BLK, HD), bf16),
            pltpu.VMEM((levels, BLK, HD), bf16),
            pltpu.VMEM((tiles, BLK, HD), bf16),
            pltpu.VMEM((tiles, BLK, HD), bf16),
            pltpu.VMEM((shard_rows, HD), bf16),
            sem((levels,)),
            sem((levels,)),
            sem((levels,)),
            sem((levels,)),
            sem((n_head,)),
            sem((n_head,)),
            sem((levels,)),
            sem((levels,)),
            sem((tiles,)),
            sem((tiles,)),
            sem((n_head,)),
            sem((n_head,)),
        ],
        compiler_params=pltpu.CompilerParams(
            collective_id=0, has_side_effects=True, vmem_limit_bytes=VMEM_LIMIT
        ),
        cost_estimate=pl.CostEstimate(
            flops=10 * elements * HD, bytes_accessed=4 * 2**20, transcendentals=elements
        ),
    )(queries, grad_out, keys, values, block_index.T)
    return pl.pallas_call(
        hand_over,
        out_shape=tuple(jax.ShapeDtypeStruct(x.shape, x.dtype) for x in results),
        in_specs=[hbm] * 3,
        out_specs=(hbm,) * 3,
        scratch_shapes=[pltpu.VMEM(x.shape, x.dtype) for x in results] + [sem((3,)), sem((3,))],
        compiler_params=pltpu.CompilerParams(vmem_limit_bytes=VMEM_LIMIT),
    )(*results)


def solution(mesh):
    placed = (P("ctx", "head"), P("ctx", None), P("ctx", None), P("ctx", "head"), P())
    return jax.shard_map(
        on_device,
        mesh=mesh,
        in_specs=placed,
        out_specs=(P(("ctx", "head"), None), P(("ctx", "head"), None), P(("ctx", "head"), None)),
        check_vma=False,
    )
```

```python
import functools

import jax
import jax.numpy as jnp
from jax import lax
from jax.experimental import pallas as pl
from jax.experimental.pallas import tpu as pltpu
from jax.sharding import PartitionSpec as P

HD = 128
BLK = 256
VMEM_LIMIT = 60 * 2**20
LOG2E = 1.4426950408889634
MESH = pl.DeviceIdType.MESH

def dot(a, b):
    return jnp.dot(a, b, preferred_element_type=jnp.float32)


def kernel(
    sizes,
    q_hbm,
    do_hbm,
    k_hbm,
    v_hbm,
    index_hbm,
    dq_out,
    gk_out,
    gv_out,
    q_ref,
    do_ref,
    index_ref,
    in_sem,
    q_t,
    do_t,
    own_kv,
    own_kt,
    part_kt,
    kv_send,
    kv_recv,
    s_tile,
    w_own,
    dp_own,
    w_part,
    dp_part,
    dq_part,
    acc,
    acc_part,
    ret_send,
    ret_recv,
    dq_stage,
    part_send,
    part_recv,
    own_send,
    own_recv,
    final,
    kv_ssem,
    kv_rsem,
    ret_ssem,
    ret_rsem,
    dq_ssem,
    dq_rsem,
    part_ssem,
    part_rsem,
    own_ssem,
    own_rsem,
    fin_ssem,
    fin_rsem,
):
    n_ctx, n_head, kv_heads, local_heads, shard_rows, levels = sizes
    repl = n_head // kv_heads
    rows_out = shard_rows // n_head
    tiles = shard_rows // BLK
    cols = local_heads * BLK
    width = local_heads * HD
    scale = HD ** (-0.5)
    c2 = scale * LOG2E
    ctx = lax.axis_index("ctx")
    head = lax.axis_index("head")
    group = head // repl
    member = head % repl
    gcol = pl.multiple_of(group * HD, HD)
    mate = group * repl + (1 - member)
    mcol = pl.multiple_of(member * HD, HD)
    ocol = pl.multiple_of((1 - member) * HD, HD)

    loads = [
        pltpu.make_async_copy(src, dst, in_sem.at[number])
        for number, (src, dst) in enumerate(
            (
                (k_hbm.at[:, pl.ds(gcol, HD)], own_kv.at[:, :HD]),
                (v_hbm.at[:, pl.ds(gcol, HD)], own_kv.at[:, HD:]),
                (index_hbm, index_ref),
                (q_hbm, q_ref),
                (do_hbm, do_ref),
            )
        )
    ]
    for load in loads:
        load.start()

    barrier = pltpu.get_barrier_semaphore()
    greet = n_head - 1
    for level in range(levels):
        step = 2**level

        @pl.when(ctx + step < n_ctx)
        def _():
            pl.semaphore_signal(barrier, inc=1, device_id=(ctx + step, head), device_id_type=MESH)

        @pl.when(ctx >= step)
        def _():
            pl.semaphore_signal(barrier, inc=1, device_id=(ctx - step, head), device_id_type=MESH)

        greet = greet + jnp.where(ctx + step < n_ctx, 1, 0) + jnp.where(ctx >= step, 1, 0)
    for off in range(1, n_head):
        pl.semaphore_signal(
            barrier, inc=1, device_id=(ctx, (head + off) % n_head), device_id_type=MESH
        )

    for load in loads[:3]:
        load.wait()
    blocks = []

    def is_block(level, block):
        return (blocks[level] == block).astype(jnp.float32)

    for level in range(levels):
        target = jnp.minimum(ctx + 2**level, n_ctx - 1)
        blocks.append(index_ref[level, target])
        chosen = jnp.zeros((BLK, 2 * HD), jnp.float32)
        for block in range(tiles):
            piece = own_kv[block * BLK : (block + 1) * BLK, :].astype(jnp.float32)
            chosen = chosen + piece * is_block(level, block)
        kv_send[level] = chosen.astype(jnp.bfloat16)

    pl.semaphore_wait(barrier, greet)

    def kv_copy(level):
        return pltpu.make_async_remote_copy(
            src_ref=kv_send.at[level],
            dst_ref=kv_recv.at[level],
            send_sem=kv_ssem.at[level],
            recv_sem=kv_rsem.at[level],
            device_id=(jnp.minimum(ctx + 2**level, n_ctx - 1), head),
            device_id_type=MESH,
        )

    for level in reversed(range(levels)):

        @pl.when(ctx + 2**level < n_ctx)
        def _():
            kv_copy(level).start()

        @pl.when(ctx < 2**level)
        def _():
            kv_recv[level] = jnp.zeros((BLK, 2 * HD), jnp.bfloat16)

        @pl.when(ctx + 2**level >= n_ctx)
        def _():
            ret_recv[level] = jnp.zeros((BLK, HD), jnp.bfloat16)

    def stacked(ref, tile):
        rows = pl.ds(tile * BLK, BLK)
        return jnp.concatenate(
            [ref[rows, h * HD : (h + 1) * HD] for h in range(local_heads)], axis=0
        )

    def slot(tile, block):
        return tile * (tile + 1) // 2 + block

    order = []
    for tile in range((tiles + 1) // 2):
        order += [tiles - 1 - tile] + ([tile] if tile != tiles - 1 - tile else [])
    early = len(order) // 2
    key_pos = lax.broadcasted_iota(jnp.int32, (BLK, cols), 0)
    query_pos = lax.broadcasted_iota(jnp.int32, (BLK, cols), 1) % BLK
    for load in loads[3:]:
        load.wait()
    for block in range(tiles):
        rows = pl.ds(block * BLK, BLK)
        own_kt[:, rows] = own_kv[rows, :HD].T

    own_stats = {}
    for tile in order:
        q_t[tile] = stacked(q_ref, tile).T
        do_t[tile] = stacked(do_ref, tile).T
    for tile in order:
        q_cat, do_cat = stacked(q_ref, tile), stacked(do_ref, tile)
        top = None
        for block in range(tile + 1):
            s = dot(own_kv[block * BLK : (block + 1) * BLK, :HD], q_t[tile])
            if block == tile:
                s = jnp.where(key_pos <= query_pos, s, -1e30)
            s_tile[block] = s
            high = jnp.max(s, axis=0, keepdims=True)
            top = high if top is None else jnp.maximum(top, high)
        top = top * c2
        total = jnp.zeros((1, cols), jnp.float32)
        mixed = jnp.zeros((1, cols), jnp.float32)
        for block in range(tile + 1):
            w = jnp.exp2(s_tile[block] * c2 - top)
            dp = dot(own_kv[block * BLK : (block + 1) * BLK, HD:], do_t[tile])
            w_own[slot(tile, block)] = w.astype(jnp.bfloat16)
            dp_own[slot(tile, block)] = dp
            total = total + jnp.sum(w, axis=0, keepdims=True)
            mixed = mixed + jnp.sum(w * dp, axis=0, keepdims=True)
        own_stats[tile] = (top, total, mixed)

    for level in range(levels):

        @pl.when(ctx >= 2**level)
        def _():
            kv_copy(level).wait_recv()

    dead = []
    for level in range(levels):
        part_kt[:, level * BLK : (level + 1) * BLK] = kv_recv[level, :, :HD].T
        dead.append(jnp.where(ctx >= 2**level, 0.0, 1e30).astype(jnp.float32))

    final_stats = {}

    def partner_part(tile):
        q_cat, do_cat = stacked(q_ref, tile), stacked(do_ref, tile)
        top_own, total_own, mixed_own = own_stats[tile]
        top = top_own
        for level in range(levels):
            s = dot(kv_recv[level, :, :HD], q_t[tile])
            s_tile[level] = s
            top = jnp.maximum(top, jnp.max(s, axis=0, keepdims=True) * c2 - dead[level])
        keep = jnp.exp2(top_own - top)
        total = total_own * keep
        mixed = mixed_own * keep
        for level in range(levels):
            w = jnp.exp2(s_tile[level] * c2 - (top + dead[level]))
            dp = dot(kv_recv[level, :, HD:], do_t[tile])
            w_part[level] = w.astype(jnp.bfloat16)
            dp_part[level] = dp
            total = total + jnp.sum(w, axis=0, keepdims=True)
            mixed = mixed + jnp.sum(w * dp, axis=0, keepdims=True)
        inverse = 1.0 / total
        delta = mixed * inverse
        inverse_low = inverse.astype(jnp.bfloat16)
        final_stats[tile] = ((keep * inverse).astype(jnp.bfloat16), delta)
        dq_t = None
        for level in range(levels):
            p = w_part[level] * inverse_low
            ds = p * (dp_part[level] - delta).astype(jnp.bfloat16)
            d_value = dot(p, do_cat)
            d_key = dot(ds, q_cat)
            if tile == order[0]:
                acc_part[level, :, :HD] = d_key
                acc_part[level, :, HD:] = d_value
            else:
                acc_part[level, :, :HD] += d_key
                acc_part[level, :, HD:] += d_value
            piece = dot(part_kt[:, level * BLK : (level + 1) * BLK], ds)
            dq_t = piece if dq_t is None else dq_t + piece
        dq_part[tile] = dq_t

    def part_copy(level):
        return pltpu.make_async_remote_copy(
            src_ref=part_send.at[level],
            dst_ref=part_recv.at[level],
            send_sem=part_ssem.at[level],
            recv_sem=part_rsem.at[level],
            device_id=(ctx, mate),
            device_id_type=MESH,
        )

    def own_copy(block):
        return pltpu.make_async_remote_copy(
            src_ref=own_send.at[block],
            dst_ref=own_recv.at[block],
            send_sem=own_ssem.at[block],
            recv_sem=own_rsem.at[block],
            device_id=(ctx, mate),
            device_id_type=MESH,
        )

    def send_partner():
        for level in reversed(range(levels)):

            @pl.when(ctx >= 2**level)
            def _():
                part_send[level] = acc_part[level, :, pl.ds(ocol, HD)].astype(jnp.bfloat16)
                part_copy(level).start()

    def return_partner():
        for level in reversed(range(levels)):

            @pl.when(ctx >= 2**level)
            def _():
                part_copy(level).wait_recv()
                ret_send[level] = (
                    acc_part[level, :, pl.ds(mcol, HD)] + part_recv[level].astype(jnp.float32)
                ).astype(jnp.bfloat16)
                ret_copy(level).start()

    def send_own(block):
        rows = slice(block * BLK, (block + 1) * BLK)
        own_send[block] = acc[rows, pl.ds(ocol, HD)].astype(jnp.bfloat16)
        own_copy(block).start()

    def ret_copy(level):
        return pltpu.make_async_remote_copy(
            src_ref=ret_send.at[level],
            dst_ref=ret_recv.at[level],
            send_sem=ret_ssem.at[level],
            recv_sem=ret_rsem.at[level],
            device_id=(jnp.maximum(ctx - 2**level, 0), head),
            device_id_type=MESH,
        )

    def dq_copy(dest, source):
        return pltpu.make_async_remote_copy(
            src_ref=dq_stage.at[pl.ds(dest * rows_out, rows_out), :],
            dst_ref=dq_out.at[:, pl.ds(pl.multiple_of(source * width, width), width)],
            send_sem=dq_ssem.at[dest],
            recv_sem=dq_rsem.at[source],
            device_id=(ctx, dest),
            device_id_type=MESH,
        )

    def dq_keep(dest):
        return pltpu.make_async_copy(
            dq_stage.at[pl.ds(dest * rows_out, rows_out), :],
            dq_out.at[:, pl.ds(pl.multiple_of(head * width, width), width)],
            dq_ssem.at[dest],
        )

    def own_part(tile):
        q_cat, do_cat = stacked(q_ref, tile), stacked(do_ref, tile)
        inverse_low, delta = final_stats[tile]
        dq_t = dq_part[tile]
        for block in range(tile + 1):
            p = w_own[slot(tile, block)] * inverse_low
            ds = p * (dp_own[slot(tile, block)] - delta).astype(jnp.bfloat16)
            d_value = dot(p, do_cat)
            d_key = dot(ds, q_cat)
            rows = slice(block * BLK, (block + 1) * BLK)
            if tile == order[0]:
                acc[rows, :HD] = d_key
                acc[rows, HD:] = d_value
            else:
                acc[rows, :HD] += d_key
                acc[rows, HD:] += d_value
            dq_t = dq_t + dot(own_kt[:, rows], ds)
        dq_t = dq_t * scale
        for h in range(local_heads):
            dq_stage[tile * BLK : (tile + 1) * BLK, h * HD : (h + 1) * HD] = (
                dq_t[:, h * BLK : (h + 1) * BLK].T.astype(jnp.bfloat16)
            )
        for dest in range(tile * BLK // rows_out, (tile + 1) * BLK // rows_out):

            @pl.when(head != dest)
            def _():
                dq_copy(dest, head).start()

            @pl.when(head == dest)
            def _():
                dq_keep(dest).start()

    last_use = [max(order.index(tile) for tile in range(block, tiles)) for block in range(tiles)]

    def finish(number):
        own_part(order[number])
        for block in reversed(range(tiles)):
            if last_use[block] == number:
                send_own(block)

    for number in range(early):
        partner_part(order[number])
        finish(number)
    for number in range(early, tiles):
        partner_part(order[number])
    send_partner()
    for number in range(early, tiles):
        finish(number)
    return_partner()

    for level in range(levels):

        @pl.when(ctx + 2**level < n_ctx)
        def _():
            ret_copy(level).wait_recv()

    factor = jnp.where(member == 0, scale, 1.0).astype(jnp.float32)

    def fin_copy(part, dest, source):
        out = (gk_out, gv_out)[part]
        return pltpu.make_async_remote_copy(
            src_ref=final.at[pl.ds(dest * rows_out, rows_out), :],
            dst_ref=out.at[:, pl.ds(pl.multiple_of(source // repl * HD, HD), HD)],
            send_sem=fin_ssem.at[dest],
            recv_sem=fin_rsem.at[source],
            device_id=(ctx, dest),
            device_id_type=MESH,
        )

    def fin_keep(part, dest):
        out = (gk_out, gv_out)[part]
        return pltpu.make_async_copy(
            final.at[pl.ds(dest * rows_out, rows_out), :],
            out.at[:, pl.ds(gcol, HD)],
            fin_ssem.at[dest],
        )

    for block in reversed(range(tiles)):
        rows = slice(block * BLK, (block + 1) * BLK)
        own_copy(block).wait_recv()
        value = acc[rows, pl.ds(mcol, HD)] + own_recv[block].astype(jnp.float32)
        for level in range(levels):
            value = value + ret_recv[level].astype(jnp.float32) * is_block(level, block)
        final[rows, :] = (value * factor).astype(jnp.bfloat16)
        for dest in range(block * BLK // rows_out, (block + 1) * BLK // rows_out):
            for part in range(2):

                @pl.when((head != dest) & (member == part))
                def _():
                    fin_copy(part, dest, head).start()

                @pl.when((head == dest) & (member == part))
                def _():
                    fin_keep(part, dest).start()

    for level in range(levels):

        @pl.when(ctx + 2**level < n_ctx)
        def _():
            kv_copy(level).wait_send()

        @pl.when(ctx >= 2**level)
        def _():
            ret_copy(level).wait_send()

    for level in range(levels):

        @pl.when(ctx >= 2**level)
        def _():
            part_copy(level).wait_send()

    for block in range(tiles):
        own_copy(block).wait_send()
    for other in range(n_head):

        @pl.when(head != other)
        def _():
            dq_copy(other, other).wait_send()
            dq_copy(other, other).wait_recv()
            fin_copy(0, other, other).wait_send()
            fin_copy(0, other, other).wait_recv()

        @pl.when(head == other)
        def _():
            dq_keep(other).wait()
            fin_keep(0, other).wait()


def hand_over(a_in, b_in, c_in, a_out, b_out, c_out, a_mid, b_mid, c_mid, in_sems, out_sems):
    mids = (a_mid, b_mid, c_mid)
    loads = [
        pltpu.make_async_copy(src, dst, in_sems.at[number])
        for number, (src, dst) in enumerate(zip((a_in, b_in, c_in), mids))
    ]
    stores = [
        pltpu.make_async_copy(src, dst, out_sems.at[number])
        for number, (src, dst) in enumerate(zip(mids, (a_out, b_out, c_out)))
    ]
    for load in loads:
        load.start()
    for load, store in zip(loads, stores):
        load.wait()
        store.start()
    for store in stores:
        store.wait()


def on_device(queries, keys, values, grad_out, block_index):
    shard_rows, q_width = queries.shape
    n_ctx = lax.axis_size("ctx")
    n_head = lax.axis_size("head")
    local_heads = q_width // HD
    kv_heads = keys.shape[1] // HD
    levels = n_ctx.bit_length() - 1
    rows_out = shard_rows // n_head
    tiles = shard_rows // BLK
    cols = local_heads * BLK
    pairs = tiles * (tiles + 1) // 2
    sizes = (n_ctx, n_head, kv_heads, local_heads, shard_rows, levels)
    bf16, f32 = jnp.bfloat16, jnp.float32
    hbm = pl.BlockSpec(memory_space=pltpu.HBM)
    sem = pltpu.SemaphoreType.DMA
    elements = cols * BLK * (pairs + tiles * levels)
    results = pl.pallas_call(
        functools.partial(kernel, sizes),
        out_shape=(
            jax.ShapeDtypeStruct((rows_out, n_head * q_width), bf16),
            jax.ShapeDtypeStruct((rows_out, kv_heads * HD), bf16),
            jax.ShapeDtypeStruct((rows_out, kv_heads * HD), bf16),
        ),
        in_specs=[hbm] * 5,
        out_specs=(hbm,) * 3,
        scratch_shapes=[
            pltpu.VMEM((shard_rows, q_width), bf16),
            pltpu.VMEM((shard_rows, q_width), bf16),
            pltpu.SMEM((levels, n_ctx), jnp.int32),
            sem((5,)),
            pltpu.VMEM((tiles, HD, cols), bf16),
            pltpu.VMEM((tiles, HD, cols), bf16),
            pltpu.VMEM((shard_rows, 2 * HD), bf16),
            pltpu.VMEM((HD, shard_rows), bf16),
            pltpu.VMEM((HD, levels * BLK), bf16),
            pltpu.VMEM((levels, BLK, 2 * HD), bf16),
            pltpu.VMEM((levels, BLK, 2 * HD), bf16),
            pltpu.VMEM((max(tiles, levels), BLK, cols), f32),
            pltpu.VMEM((pairs, BLK, cols), bf16),
            pltpu.VMEM((pairs, BLK, cols), f32),
            pltpu.VMEM((levels, BLK, cols), bf16),
            pltpu.VMEM((levels, BLK, cols), f32),
            pltpu.VMEM((tiles, HD, cols), f32),
            pltpu.VMEM((shard_rows, 2 * HD), f32),
            pltpu.VMEM((levels, BLK, 2 * HD), f32),
            pltpu.VMEM((levels, BLK, HD), bf16),
            pltpu.VMEM((levels, BLK, HD), bf16),
            pltpu.VMEM((shard_rows, q_width), bf16),
            pltpu.VMEM((levels, BLK, HD), bf16),
            pltpu.VMEM((levels, BLK, HD), bf16),
            pltpu.VMEM((tiles, BLK, HD), bf16),
            pltpu.VMEM((tiles, BLK, HD), bf16),
            pltpu.VMEM((shard_rows, HD), bf16),
            sem((levels,)),
            sem((levels,)),
            sem((levels,)),
            sem((levels,)),
            sem((n_head,)),
            sem((n_head,)),
            sem((levels,)),
            sem((levels,)),
            sem((tiles,)),
            sem((tiles,)),
            sem((n_head,)),
            sem((n_head,)),
        ],
        compiler_params=pltpu.CompilerParams(
            collective_id=0, has_side_effects=True, vmem_limit_bytes=VMEM_LIMIT
        ),
        cost_estimate=pl.CostEstimate(
            flops=10 * elements * HD, bytes_accessed=4 * 2**20, transcendentals=elements
        ),
    )(queries, grad_out, keys, values, block_index.T)
    return pl.pallas_call(
        hand_over,
        out_shape=tuple(jax.ShapeDtypeStruct(x.shape, x.dtype) for x in results),
        in_specs=[hbm] * 3,
        out_specs=(hbm,) * 3,
        scratch_shapes=[pltpu.VMEM(x.shape, x.dtype) for x in results] + [sem((3,)), sem((3,))],
        compiler_params=pltpu.CompilerParams(vmem_limit_bytes=VMEM_LIMIT),
    )(*results)


def solution(mesh):
    placed = (P("ctx", "head"), P("ctx", None), P("ctx", None), P("ctx", "head"), P())
    return jax.shard_map(
        on_device,
        mesh=mesh,
        in_specs=placed,
        out_specs=(P(("ctx", "head"), None), P(("ctx", "head"), None), P(("ctx", "head"), None)),
        check_vma=False,
    )
```

```python
import functools

import jax
import jax.numpy as jnp
from jax import lax
from jax.experimental import pallas as pl
from jax.experimental.pallas import tpu as pltpu
from jax.sharding import PartitionSpec as P

HD = 128
BLK = 256
VMEM_LIMIT = 60 * 2**20
LOG2E = 1.4426950408889634
MESH = pl.DeviceIdType.MESH

def dot(a, b):
    return jnp.dot(a, b, preferred_element_type=jnp.float32)


def kernel(
    sizes,
    q_hbm,
    do_hbm,
    k_hbm,
    v_hbm,
    index_hbm,
    dq_out,
    gk_out,
    gv_out,
    q_ref,
    do_ref,
    index_ref,
    in_sem,
    q_t,
    do_t,
    own_kv,
    own_kt,
    part_kt,
    kv_send,
    kv_recv,
    s_tile,
    w_own,
    dp_own,
    w_part,
    dp_part,
    dq_part,
    acc,
    acc_part,
    ret_send,
    ret_recv,
    dq_stage,
    pair_send,
    pair_recv,
    final,
    kv_ssem,
    kv_rsem,
    relay_ssem,
    relay_rsem,
    ret_ssem,
    ret_rsem,
    dq_ssem,
    dq_rsem,
    pair_ssem,
    pair_rsem,
    fin_ssem,
    fin_rsem,
):
    n_ctx, n_head, kv_heads, local_heads, shard_rows, levels = sizes
    repl = n_head // kv_heads
    per_member = n_head // repl
    rows_out = shard_rows // n_head
    tiles = shard_rows // BLK
    cols = local_heads * BLK
    width = local_heads * HD
    scale = HD ** (-0.5)
    c2 = scale * LOG2E
    ctx = lax.axis_index("ctx")
    head = lax.axis_index("head")
    group = head // repl
    member = head % repl
    gcol = pl.multiple_of(group * HD, HD)
    half = BLK // repl
    my_half = pl.multiple_of(member * half, half)
    mate = group * repl + (member + 1) % repl

    loads = [
        pltpu.make_async_copy(src, dst, in_sem.at[number])
        for number, (src, dst) in enumerate(
            (
                (k_hbm.at[:, pl.ds(gcol, HD)], own_kv.at[:, :HD]),
                (v_hbm.at[:, pl.ds(gcol, HD)], own_kv.at[:, HD:]),
                (index_hbm, index_ref),
                (q_hbm, q_ref),
                (do_hbm, do_ref),
            )
        )
    ]
    for load in loads:
        load.start()

    barrier = pltpu.get_barrier_semaphore()
    greet = n_head - 1
    for level in range(levels):
        step = 2**level

        @pl.when(ctx + step < n_ctx)
        def _():
            pl.semaphore_signal(barrier, inc=1, device_id=(ctx + step, head), device_id_type=MESH)

        @pl.when(ctx >= step)
        def _():
            pl.semaphore_signal(barrier, inc=1, device_id=(ctx - step, head), device_id_type=MESH)

        greet = greet + jnp.where(ctx + step < n_ctx, 1, 0) + jnp.where(ctx >= step, 1, 0)
    for off in range(1, n_head):
        pl.semaphore_signal(
            barrier, inc=1, device_id=(ctx, (head + off) % n_head), device_id_type=MESH
        )

    for load in loads[:3]:
        load.wait()
    blocks = []

    def is_block(level, block):
        return (blocks[level] == block).astype(jnp.float32)

    for level in range(levels):
        target = jnp.minimum(ctx + 2**level, n_ctx - 1)
        blocks.append(index_ref[level, target])
        chosen = jnp.zeros((BLK, 2 * HD), jnp.float32)
        for block in range(tiles):
            piece = own_kv[block * BLK : (block + 1) * BLK, :].astype(jnp.float32)
            chosen = chosen + piece * is_block(level, block)
        kv_send[level] = chosen.astype(jnp.bfloat16)

    pl.semaphore_wait(barrier, greet)

    def kv_copy(level):
        return pltpu.make_async_remote_copy(
            src_ref=kv_send.at[level, pl.ds(my_half, half), :],
            dst_ref=kv_recv.at[level, pl.ds(my_half, half), :],
            send_sem=kv_ssem.at[level],
            recv_sem=kv_rsem.at[level],
            device_id=(jnp.minimum(ctx + 2**level, n_ctx - 1), head),
            device_id_type=MESH,
        )

    def kv_relay(level):
        return pltpu.make_async_remote_copy(
            src_ref=kv_recv.at[level, pl.ds(my_half, half), :],
            dst_ref=kv_recv.at[level, pl.ds(my_half, half), :],
            send_sem=relay_ssem.at[level],
            recv_sem=relay_rsem.at[level],
            device_id=(ctx, mate),
            device_id_type=MESH,
        )

    def relay():
        for level in reversed(range(levels)):

            @pl.when(ctx >= 2**level)
            def _():
                kv_copy(level).wait_recv()
                kv_relay(level).start()

    for level in reversed(range(levels)):

        @pl.when(ctx + 2**level < n_ctx)
        def _():
            kv_copy(level).start()

        @pl.when(ctx < 2**level)
        def _():
            kv_recv[level] = jnp.zeros((BLK, 2 * HD), jnp.bfloat16)

        @pl.when(ctx + 2**level >= n_ctx)
        def _():
            ret_recv[level] = jnp.zeros((BLK, 2 * HD), jnp.bfloat16)

    def stacked(ref, tile):
        rows = pl.ds(tile * BLK, BLK)
        return jnp.concatenate(
            [ref[rows, h * HD : (h + 1) * HD] for h in range(local_heads)], axis=0
        )

    def slot(tile, block):
        return tile * (tile + 1) // 2 + block

    order = []
    for tile in range((tiles + 1) // 2):
        order += [tiles - 1 - tile] + ([tile] if tile != tiles - 1 - tile else [])
    early = len(order) // 2
    key_pos = lax.broadcasted_iota(jnp.int32, (BLK, cols), 0)
    query_pos = lax.broadcasted_iota(jnp.int32, (BLK, cols), 1) % BLK
    for load in loads[3:]:
        load.wait()
    for block in range(tiles):
        rows = pl.ds(block * BLK, BLK)
        own_kt[:, rows] = own_kv[rows, :HD].T

    own_stats = {}
    for tile in order:
        q_t[tile] = stacked(q_ref, tile).T
        do_t[tile] = stacked(do_ref, tile).T
    for tile in order:
        q_cat, do_cat = stacked(q_ref, tile), stacked(do_ref, tile)
        top = None
        for block in range(tile + 1):
            s = dot(own_kv[block * BLK : (block + 1) * BLK, :HD], q_t[tile])
            if block == tile:
                s = jnp.where(key_pos <= query_pos, s, -1e30)
            s_tile[block] = s
            high = jnp.max(s, axis=0, keepdims=True)
            top = high if top is None else jnp.maximum(top, high)
        top = top * c2
        total = jnp.zeros((1, cols), jnp.float32)
        mixed = jnp.zeros((1, cols), jnp.float32)
        for block in range(tile + 1):
            w = jnp.exp2(s_tile[block] * c2 - top)
            dp = dot(own_kv[block * BLK : (block + 1) * BLK, HD:], do_t[tile])
            w_own[slot(tile, block)] = w.astype(jnp.bfloat16)
            dp_own[slot(tile, block)] = dp
            total = total + jnp.sum(w, axis=0, keepdims=True)
            mixed = mixed + jnp.sum(w * dp, axis=0, keepdims=True)
        own_stats[tile] = (top, total, mixed)
        if tile == order[early]:
            relay()

    for level in range(levels):

        @pl.when(ctx >= 2**level)
        def _():
            kv_relay(level).wait_recv()

    dead = []
    for level in range(levels):
        part_kt[:, level * BLK : (level + 1) * BLK] = kv_recv[level, :, :HD].T
        dead.append(jnp.where(ctx >= 2**level, 0.0, 1e30).astype(jnp.float32))

    final_stats = {}

    def partner_part(tile):
        q_cat, do_cat = stacked(q_ref, tile), stacked(do_ref, tile)
        top_own, total_own, mixed_own = own_stats[tile]
        top = top_own
        for level in range(levels):
            s = dot(kv_recv[level, :, :HD], q_t[tile])
            s_tile[level] = s
            top = jnp.maximum(top, jnp.max(s, axis=0, keepdims=True) * c2 - dead[level])
        keep = jnp.exp2(top_own - top)
        total = total_own * keep
        mixed = mixed_own * keep
        for level in range(levels):
            w = jnp.exp2(s_tile[level] * c2 - (top + dead[level]))
            dp = dot(kv_recv[level, :, HD:], do_t[tile])
            w_part[level] = w.astype(jnp.bfloat16)
            dp_part[level] = dp
            total = total + jnp.sum(w, axis=0, keepdims=True)
            mixed = mixed + jnp.sum(w * dp, axis=0, keepdims=True)
        inverse = 1.0 / total
        delta = mixed * inverse
        inverse_low = inverse.astype(jnp.bfloat16)
        final_stats[tile] = ((keep * inverse).astype(jnp.bfloat16), delta)
        dq_t = None
        for level in range(levels):
            p = w_part[level] * inverse_low
            ds = p * (dp_part[level] - delta).astype(jnp.bfloat16)
            d_value = dot(p, do_cat)
            d_key = dot(ds, q_cat)
            if tile == order[0]:
                acc_part[level, :, :HD] = d_key
                acc_part[level, :, HD:] = d_value
            else:
                acc_part[level, :, :HD] += d_key
                acc_part[level, :, HD:] += d_value
            piece = dot(part_kt[:, level * BLK : (level + 1) * BLK], ds)
            dq_t = piece if dq_t is None else dq_t + piece
        dq_part[tile] = dq_t

    def send_partner():
        for level in reversed(range(levels)):
            ret_send[level, :, :HD] = (acc_part[level, :, :HD] * scale).astype(jnp.bfloat16)
            ret_send[level, :, HD:] = acc_part[level, :, HD:].astype(jnp.bfloat16)

            @pl.when(ctx >= 2**level)
            def _():
                ret_copy(level).start()

    def ret_copy(level):
        return pltpu.make_async_remote_copy(
            src_ref=ret_send.at[level],
            dst_ref=ret_recv.at[level],
            send_sem=ret_ssem.at[level],
            recv_sem=ret_rsem.at[level],
            device_id=(jnp.maximum(ctx - 2**level, 0), head),
            device_id_type=MESH,
        )

    def dq_copy(dest, source):
        return pltpu.make_async_remote_copy(
            src_ref=dq_stage.at[pl.ds(dest * rows_out, rows_out), :],
            dst_ref=dq_out.at[:, pl.ds(pl.multiple_of(source * width, width), width)],
            send_sem=dq_ssem.at[dest],
            recv_sem=dq_rsem.at[source],
            device_id=(ctx, dest),
            device_id_type=MESH,
        )

    def dq_keep(dest):
        return pltpu.make_async_copy(
            dq_stage.at[pl.ds(dest * rows_out, rows_out), :],
            dq_out.at[:, pl.ds(pl.multiple_of(head * width, width), width)],
            dq_ssem.at[dest],
        )

    def own_part(tile):
        q_cat, do_cat = stacked(q_ref, tile), stacked(do_ref, tile)
        inverse_low, delta = final_stats[tile]
        dq_t = dq_part[tile]
        for block in range(tile + 1):
            p = w_own[slot(tile, block)] * inverse_low
            ds = p * (dp_own[slot(tile, block)] - delta).astype(jnp.bfloat16)
            d_value = dot(p, do_cat)
            d_key = dot(ds, q_cat)
            rows = slice(block * BLK, (block + 1) * BLK)
            if tile == order[0]:
                acc[rows, :HD] = d_key
                acc[rows, HD:] = d_value
            else:
                acc[rows, :HD] += d_key
                acc[rows, HD:] += d_value
            dq_t = dq_t + dot(own_kt[:, rows], ds)
        dq_t = dq_t * scale
        for h in range(local_heads):
            dq_stage[tile * BLK : (tile + 1) * BLK, h * HD : (h + 1) * HD] = (
                dq_t[:, h * BLK : (h + 1) * BLK].T.astype(jnp.bfloat16)
            )
        for dest in range(tile * BLK // rows_out, (tile + 1) * BLK // rows_out):

            @pl.when(head != dest)
            def _():
                dq_copy(dest, head).start()

            @pl.when(head == dest)
            def _():
                dq_keep(dest).start()

    for tile in order[:early]:
        partner_part(tile)
        own_part(tile)
    for tile in order[early:]:
        partner_part(tile)
    send_partner()
    for tile in order[early:]:
        own_part(tile)

    for level in range(levels):

        @pl.when(ctx + 2**level < n_ctx)
        def _():
            ret_copy(level).wait_recv()

    for block in range(tiles):
        rows = slice(block * BLK, (block + 1) * BLK)
        value = jnp.concatenate([acc[rows, :HD] * scale, acc[rows, HD:]], axis=1)
        for level in range(levels):
            back = ret_recv[level].astype(jnp.float32)
            value = value + back * is_block(level, block)
        acc[rows, :] = value

    def pair_copy(off, k):
        return pltpu.make_async_remote_copy(
            src_ref=pair_send.at[off - 1, k],
            dst_ref=pair_recv.at[off - 1, k],
            send_sem=pair_ssem.at[off - 1, k],
            recv_sem=pair_rsem.at[off - 1, k],
            device_id=(ctx, group * repl + (member + off) % repl),
            device_id_type=MESH,
        )

    for k in range(per_member):
        for off in range(1, repl):
            begin = pl.multiple_of((k * repl + (member + off) % repl) * rows_out, rows_out)
            pair_send[off - 1, k] = acc[pl.ds(begin, rows_out), :].astype(jnp.bfloat16)
            pair_copy(off, k).start()

    def fin_copy(part, k, source_group):
        out = (gk_out, gv_out)[part]
        return pltpu.make_async_remote_copy(
            src_ref=final.at[part, k],
            dst_ref=out.at[:, pl.ds(pl.multiple_of(source_group * HD, HD), HD)],
            send_sem=fin_ssem.at[part, k],
            recv_sem=fin_rsem.at[part, source_group],
            device_id=(ctx, k * repl + member),
            device_id_type=MESH,
        )

    def fin_keep(part, k):
        out = (gk_out, gv_out)[part]
        return pltpu.make_async_copy(
            final.at[part, k], out.at[:, pl.ds(gcol, HD)], fin_ssem.at[part, k]
        )

    for k in range(per_member):
        begin = pl.multiple_of((k * repl + member) * rows_out, rows_out)
        value = acc[pl.ds(begin, rows_out), :]
        for off in range(1, repl):
            pair_copy(off, k).wait_recv()
            value = value + pair_recv[off - 1, k].astype(jnp.float32)
        final[0, k] = value[:, :HD].astype(jnp.bfloat16)
        final[1, k] = value[:, HD:].astype(jnp.bfloat16)

        @pl.when(group != k)
        def _():
            fin_copy(0, k, group).start()
            fin_copy(1, k, group).start()

        @pl.when(group == k)
        def _():
            fin_keep(0, k).start()
            fin_keep(1, k).start()

    for level in range(levels):

        @pl.when(ctx + 2**level < n_ctx)
        def _():
            kv_copy(level).wait_send()

        @pl.when(ctx >= 2**level)
        def _():
            ret_copy(level).wait_send()
            kv_relay(level).wait_send()

    for k in range(per_member):
        for off in range(1, repl):
            pair_copy(off, k).wait_send()
    for other in range(n_head):

        @pl.when(head != other)
        def _():
            dq_copy(other, other).wait_send()
            dq_copy(other, other).wait_recv()

        @pl.when(head == other)
        def _():
            dq_keep(other).wait()

    for k in range(kv_heads):

        @pl.when(group != k)
        def _():
            for part in range(2):
                fin_copy(part, k, k).wait_send()
                fin_copy(part, k, k).wait_recv()

        @pl.when(group == k)
        def _():
            for part in range(2):
                fin_keep(part, k).wait()


def hand_over(a_in, b_in, c_in, a_out, b_out, c_out, a_mid, b_mid, c_mid, in_sems, out_sems):
    mids = (a_mid, b_mid, c_mid)
    loads = [
        pltpu.make_async_copy(src, dst, in_sems.at[number])
        for number, (src, dst) in enumerate(zip((a_in, b_in, c_in), mids))
    ]
    stores = [
        pltpu.make_async_copy(src, dst, out_sems.at[number])
        for number, (src, dst) in enumerate(zip(mids, (a_out, b_out, c_out)))
    ]
    for load in loads:
        load.start()
    for load, store in zip(loads, stores):
        load.wait()
        store.start()
    for store in stores:
        store.wait()


def on_device(queries, keys, values, grad_out, block_index):
    shard_rows, q_width = queries.shape
    n_ctx = lax.axis_size("ctx")
    n_head = lax.axis_size("head")
    local_heads = q_width // HD
    kv_heads = keys.shape[1] // HD
    levels = n_ctx.bit_length() - 1
    repl = n_head // kv_heads
    rows_out = shard_rows // n_head
    tiles = shard_rows // BLK
    cols = local_heads * BLK
    pairs = tiles * (tiles + 1) // 2
    sizes = (n_ctx, n_head, kv_heads, local_heads, shard_rows, levels)
    bf16, f32 = jnp.bfloat16, jnp.float32
    hbm = pl.BlockSpec(memory_space=pltpu.HBM)
    sem = pltpu.SemaphoreType.DMA
    elements = cols * BLK * (pairs + tiles * levels)
    results = pl.pallas_call(
        functools.partial(kernel, sizes),
        out_shape=(
            jax.ShapeDtypeStruct((rows_out, n_head * q_width), bf16),
            jax.ShapeDtypeStruct((rows_out, kv_heads * HD), bf16),
            jax.ShapeDtypeStruct((rows_out, kv_heads * HD), bf16),
        ),
        in_specs=[hbm] * 5,
        out_specs=(hbm,) * 3,
        scratch_shapes=[
            pltpu.VMEM((shard_rows, q_width), bf16),
            pltpu.VMEM((shard_rows, q_width), bf16),
            pltpu.SMEM((levels, n_ctx), jnp.int32),
            sem((5,)),
            pltpu.VMEM((tiles, HD, cols), bf16),
            pltpu.VMEM((tiles, HD, cols), bf16),
            pltpu.VMEM((shard_rows, 2 * HD), bf16),
            pltpu.VMEM((HD, shard_rows), bf16),
            pltpu.VMEM((HD, levels * BLK), bf16),
            pltpu.VMEM((levels, BLK, 2 * HD), bf16),
            pltpu.VMEM((levels, BLK, 2 * HD), bf16),
            pltpu.VMEM((max(tiles, levels), BLK, cols), f32),
            pltpu.VMEM((pairs, BLK, cols), bf16),
            pltpu.VMEM((pairs, BLK, cols), f32),
            pltpu.VMEM((levels, BLK, cols), bf16),
            pltpu.VMEM((levels, BLK, cols), f32),
            pltpu.VMEM((tiles, HD, cols), f32),
            pltpu.VMEM((shard_rows, 2 * HD), f32),
            pltpu.VMEM((levels, BLK, 2 * HD), f32),
            pltpu.VMEM((levels, BLK, 2 * HD), bf16),
            pltpu.VMEM((levels, BLK, 2 * HD), bf16),
            pltpu.VMEM((shard_rows, q_width), bf16),
            pltpu.VMEM((max(repl - 1, 1), kv_heads, rows_out, 2 * HD), bf16),
            pltpu.VMEM((max(repl - 1, 1), kv_heads, rows_out, 2 * HD), bf16),
            pltpu.VMEM((2, kv_heads, rows_out, HD), bf16),
            sem((levels,)),
            sem((levels,)),
            sem((levels,)),
            sem((levels,)),
            sem((levels,)),
            sem((levels,)),
            sem((n_head,)),
            sem((n_head,)),
            sem((max(repl - 1, 1), kv_heads)),
            sem((max(repl - 1, 1), kv_heads)),
            sem((2, kv_heads)),
            sem((2, kv_heads)),
        ],
        compiler_params=pltpu.CompilerParams(
            collective_id=0, has_side_effects=True, vmem_limit_bytes=VMEM_LIMIT
        ),
        cost_estimate=pl.CostEstimate(
            flops=10 * elements * HD, bytes_accessed=4 * 2**20, transcendentals=elements
        ),
    )(queries, grad_out, keys, values, block_index.T)
    return pl.pallas_call(
        hand_over,
        out_shape=tuple(jax.ShapeDtypeStruct(x.shape, x.dtype) for x in results),
        in_specs=[hbm] * 3,
        out_specs=(hbm,) * 3,
        scratch_shapes=[pltpu.VMEM(x.shape, x.dtype) for x in results] + [sem((3,)), sem((3,))],
        compiler_params=pltpu.CompilerParams(vmem_limit_bytes=VMEM_LIMIT),
    )(*results)


def solution(mesh):
    placed = (P("ctx", "head"), P("ctx", None), P("ctx", None), P("ctx", "head"), P())
    return jax.shard_map(
        on_device,
        mesh=mesh,
        in_specs=placed,
        out_specs=(P(("ctx", "head"), None), P(("ctx", "head"), None), P(("ctx", "head"), None)),
        check_vma=False,
    )
```
